512 devices in a mesh: seq: 8 (over y), exp: 16 (over z, core), tp: 4 (over x).
Axes of the slice: x: 4, y: 8, z: 8, core: 2. Of those that a mesh axis runs over, the one named last changes fastest.
Arguments:
- tokens: bfloat16 [4096, 4096], P(('seq', 'exp'), 'tp'), may hold values from -6 to 6
- expert_ids: int32 [4096, 8], P(('seq', 'exp')), may hold values from 0 to 15, all different within a row; in each aligned block of 32 rows (0 to 31, 32 to 63, ...) at most 24 rows name the same one
- route_weights: float32 [4096, 8], P(('seq', 'exp')), may hold values from 0.05 to 1
- expert_gate: bfloat16 [16, 4096, 512], P('exp', None, 'tp'), may hold values from -0.09375 to 0.09375
- expert_up: bfloat16 [16, 4096, 512], P('exp', None, 'tp'), may hold values from -0.09375 to 0.09375
- expert_down: bfloat16 [16, 512, 4096], P('exp', None, 'tp'), may hold values from -0.25 to 0.25
- student_gate: bfloat16 [4096, 8192], P('seq', ('exp', 'tp')), may hold values from -0.09375 to 0.09375
- student_up: bfloat16 [4096, 8192], P('seq', ('exp', 'tp')), may hold values from -0.09375 to 0.09375
- student_down: bfloat16 [8192, 4096], P(('exp', 'tp'), 'seq'), may hold values from -0.0625 to 0.0625
- out_grad: bfloat16 [4096, 4096], P(('seq', 'exp'), 'tp'), may hold values from -6 to 6
Outputs:
- teacher_out: bfloat16 [4096, 4096], P(('seq', 'exp'), 'tp')
- grad_gate: float32 [4096, 8192], P('seq', ('exp', 'tp'))
- grad_up: float32 [4096, 8192], P('seq', ('exp', 'tp'))
- grad_down: float32 [8192, 4096], P(('exp', 'tp'), 'seq')
The draws below stay inside these ranges and needn't reach their ends.
Inputs may be any that keep to these rules, and one draw needn't show every extreme that they name: `expert_ids`: the 8 ids of a row are distinct. Among the 32 rows of one device no id appears more than 24 times, and in every draw some device's rows name some id exactly 24 times.
All inputs are finite; a program needn't handle non-finite values.
Results may differ from the reference program's by a relative error of at most 0.019.
Values may be sent and summed in bfloat16 or wider, within the bound.
A program may use at most 64 MiB of HBM per device.

```python
import math
import jax
import jax.numpy as jnp
import numpy as np
from jax import lax

D = 4096
TFF = 512
SFF = 8192
TOPK = 8
TT = 32
EXPERTS = 16
CAP = 24
GROUP = 512
TOKENS = 4096
N_SEQ = 8


def block_levels(stream_key, shape, cuts, smallest, top_value):
    level, own = 1.0, jax.random.fold_in(stream_key, 6)
    for axis_at, shards_of in cuts:
        draws = jnp.exp(jax.random.uniform(jax.random.fold_in(own, axis_at), (shards_of,), jnp.float32, smallest / len(cuts), top_value / len(cuts)))
        level = level * jnp.repeat(draws, shape[axis_at] // shards_of).reshape([-1 if axis == axis_at else 1 for axis in range(len(shape))])
    return level


def assign_block(key, own, number, rows, count, top, limit, slope):
    sequence = jax.random.permutation(key, count)
    crowded, common = load_shares(count, rows * top, limit, slope, True), load_shares(count, rows * top, limit, slope, False)
    places = jnp.arange(count)

    def named(tallies, rotation):
        used = int((tallies > 0).sum())
        fixed = max(1, used // 4)
        shifted = fixed + (places - fixed + rotation * (used - fixed)) % max(1, count - fixed)
        return jnp.zeros((count,), jnp.int32).at[sequence[jnp.where(places < fixed, places, shifted)]].set(jnp.asarray(tallies, jnp.int32))

    tallies = jnp.where(number % 4 == 0, named(crowded, number // 4), named(common, number - number // 4 - 1))
    mixed = jax.random.permutation(jax.random.fold_in(own, 3), count)
    giver, sink = mixed[0:count // 2 * 2:2], mixed[1:count // 2 * 2:2]
    slack = jnp.minimum(tallies[giver] - 1, limit - tallies[sink]) // 2
    slack = jnp.where((giver == sequence[0]) | (sink == sequence[0]) | (tallies[sink] == 0), 0, jnp.maximum(slack, 0))
    shifted = jax.random.randint(jax.random.fold_in(own, 4), (count // 2,), 0, 1 << 20) % (slack + 1)
    tallies = tallies.at[giver].add(-shifted).at[sink].add(shifted)
    members = jnp.searchsorted(jnp.cumsum(tallies), jnp.arange(rows * top), side="right").astype(jnp.int32)
    grid = members.reshape(top, rows).T
    grid = grid[jax.random.permutation(jax.random.fold_in(own, 1), rows)]
    rotation = jax.random.randint(jax.random.fold_in(own, 2), (rows, 1), 0, top)
    return jnp.take_along_axis(grid, (jnp.arange(top)[None, :] + rotation) % top, axis=1)


def load_shares(amount, total, most, skew, full):
    weights = [(1 << 20) // math.isqrt(grade ** skew) + 1 for grade in range(1, amount + 1)]
    largest = most if full else min(most, max(-(-total // amount), total * weights[0] // sum(weights)))
    least = 1 if total - largest >= amount - 1 else 0
    counts, surplus = [largest] + [least] * (amount - 1), total - largest - least * (amount - 1)
    while surplus > 0:
        free = [i for i in range(1, amount) if counts[i] < largest] or [i for i in range(1, amount) if counts[i] < most]
        whole, remaining = sum([weights[i] for i in free]), surplus
        for i in free:
            extra = min(most - counts[i], max(1, remaining * weights[i] // whole), surplus)
            counts[i] = counts[i] + extra
            surplus = surplus - extra
    return np.array(counts)


def gaussian(own_key, shape, deviation, bound, split=(), kind=jnp.bfloat16):
    entries = jax.random.normal(own_key, shape, jnp.float32) * deviation
    if len(split) > 0:
        entries = block_levels(own_key, shape, split, -0.22, 0.18) * entries
    return jnp.clip(entries, min=-bound, max=bound).astype(kind)


def setup_inputs(seed: int = 0) -> dict:
    keys = jax.random.split(jax.random.key(seed), 11)
    tokens = gaussian(keys[0], (TOKENS, D), 1.0, 6.0, ((0, 128), (1, 4)))
    expert_ids_keys = jax.random.split(jax.random.fold_in(keys[1], 1), TOKENS // TT)
    expert_ids_turns = jax.random.permutation(jax.random.fold_in(keys[1], 3), TOKENS // TT)
    expert_ids = jax.vmap(lambda own, number: assign_block(jax.random.fold_in(keys[1], 2), own, number, TT, EXPERTS, TOPK, CAP, 2))(expert_ids_keys, expert_ids_turns).reshape((TOKENS, TOPK))
    route_weights = jnp.clip(jnp.exp(math.log(1.0) - 2.9957323 * jax.random.uniform(keys[2], (TOKENS, TOPK), jnp.float32) ** block_levels(keys[2], (TOKENS, TOPK), ((0, 128),), -0.2, 0.2)), 0.05, 1.0)
    expert_gate = gaussian(keys[3], (EXPERTS, D, TFF), D ** -0.5, 0.09375, ((0, 16), (2, 4)))
    expert_up = gaussian(keys[4], (EXPERTS, D, TFF), D ** -0.5, 0.09375, ((0, 16), (2, 4)))
    expert_down = gaussian(keys[5], (EXPERTS, TFF, D), TFF ** -0.5, 0.25, ((0, 16), (2, 4)))
    student_gate = gaussian(keys[6], (D, SFF), D ** -0.5, 0.09375, ((0, 8), (1, 64)))
    student_up = gaussian(keys[7], (D, SFF), D ** -0.5, 0.09375, ((0, 8), (1, 64)))
    student_down = gaussian(keys[8], (SFF, D), SFF ** -0.5, 0.0625, ((0, 64), (1, 8)))
    out_grad = gaussian(keys[9], (TOKENS, D), 1.0, 6.0, ((0, 128), (1, 4)))
    return {"tokens": tokens, "expert_ids": expert_ids, "route_weights": route_weights, "expert_gate": expert_gate, "expert_up": expert_up, "expert_down": expert_down, "student_gate": student_gate, "student_up": student_up, "student_down": student_down, "out_grad": out_grad}


def expert_apply(rows, gate_mat, up_mat, down_mat):
    gate_sum = jnp.dot(rows, gate_mat, preferred_element_type=jnp.float32)
    up_sum = jnp.dot(rows, up_mat, preferred_element_type=jnp.float32)
    hidden = (jax.nn.silu(gate_sum) * up_sum).astype(jnp.bfloat16)
    return jnp.dot(hidden, down_mat, preferred_element_type=jnp.float32).astype(jnp.bfloat16)

def rounded(term):
    return lax.optimization_barrier(term.astype(jnp.bfloat16)).astype(jnp.float32)

def silu_grad(gate_sum):
    sigmoid_val = jax.nn.sigmoid(gate_sum)
    return sigmoid_val * (1.0 + gate_sum * (1.0 - sigmoid_val))

def reference(tokens, expert_ids, route_weights, expert_gate, expert_up, expert_down, student_gate, student_up, student_down, out_grad):
    labels = jnp.arange(EXPERTS, dtype=jnp.int32)
    chosen = expert_ids[:, :, None] == labels[None, None, :]
    coeffs = lax.optimization_barrier(jnp.sum(jnp.where(chosen, route_weights[:, :, None], jnp.zeros((), jnp.float32)), axis=1))

    def add_expert(running, packed):
        gate_mat, up_mat, down_mat, weight_col = packed
        result = expert_apply(tokens, gate_mat, up_mat, down_mat).astype(jnp.float32)
        return (running + weight_col[:, None] * result, None)
    start_sum = jnp.zeros((TOKENS, D), jnp.float32)
    running = lax.scan(add_expert, start_sum, (expert_gate, expert_up, expert_down, coeffs.T))[0]
    teacher_out = running.astype(jnp.bfloat16)
    act_groups = teacher_out.reshape(N_SEQ, GROUP, D)
    grad_groups = out_grad.reshape(N_SEQ, GROUP, D)

    def add_group(totals, packed):
        act_rows, grad_rows = packed
        gate_sum = jnp.dot(act_rows, student_gate, preferred_element_type=jnp.float32)
        up_sum = jnp.dot(act_rows, student_up, preferred_element_type=jnp.float32)
        activated = jax.nn.silu(gate_sum)
        hidden = (activated * up_sum).astype(jnp.bfloat16)
        hidden_grad = jnp.dot(grad_rows, student_down.T, preferred_element_type=jnp.float32)
        gate_grad = (hidden_grad * up_sum * silu_grad(gate_sum)).astype(jnp.bfloat16)
        up_grad = (hidden_grad * activated).astype(jnp.bfloat16)
        gate_term = jnp.dot(act_rows.T, gate_grad, preferred_element_type=jnp.float32)
        up_term = jnp.dot(act_rows.T, up_grad, preferred_element_type=jnp.float32)
        down_term = jnp.dot(hidden.T, grad_rows, preferred_element_type=jnp.float32)
        return ((totals[0] + rounded(gate_term), totals[1] + rounded(up_term), totals[2] + rounded(down_term)), None)
    zero_proj = jnp.zeros((D, SFF), jnp.float32)
    zero_down = jnp.zeros((SFF, D), jnp.float32)
    sums = lax.scan(add_group, (zero_proj, zero_proj, zero_down), (act_groups, grad_groups))[0]
    return (teacher_out, sums[0], sums[1], sums[2])
```

```python
import jax
import jax.numpy as jnp
from jax import lax
from jax.experimental import pallas as pl
from jax.experimental.pallas import tpu as pltpu
from jax.sharding import PartitionSpec as P

MESH = pl.DeviceIdType.MESH
F32 = jnp.float32
BF16 = jnp.bfloat16
Z_ORDER = (0, 1, 7, 2, 6, 3, 5, 4)
Z_POS = {z: i for i, z in enumerate(Z_ORDER)}
N_RECV = 224
N_SEND = 64


def row_of(half, z, other=0):
    return other * 256 + half * 128 + Z_POS[z % 8] * 16


def sigmoid(a):
    return 1.0 / (1.0 + jnp.exp(-a))


class Agenda:
    def __init__(self):
        self.steps = []

    def at(self, time, step):
        self.steps.append((time, len(self.steps), step))

    def run(self):
        for _, _, step in sorted(self.steps, key=lambda s: (s[0], s[1])):
            step()


def kernel(
    tokens, ids, weights, egate, eup, edown, sgate, sup, sdown, ograd,
    t_out, gg_out, gu_out, gd_out,
    tok, act, dout, wt, wed, wgu, wd, hid, coef, part, sibp, rsb, gu, hg, gt, grad, ring,
    send_sems, recv_sems, local_sems,
):
    yo = lax.axis_index("seq")
    eo = lax.axis_index("exp")
    xo = lax.axis_index("tp")
    zo = eo // 2
    co = lax.rem(eo, 2)

    def z_dev(d):
        return (yo, lax.rem(zo + d + 8, 8) * 2 + co, xo)

    def x_dev(d):
        return (yo, eo, lax.rem(xo + d + 4, 4))

    def y_dev(d):
        return (lax.rem(yo + d + 8, 8), eo, xo)

    sib = (yo, zo * 2 + (1 - co), xo)
    agenda = Agenda()
    drains = []
    counts = {"send": 0, "recv": 0, "local": 0}

    def new_send():
        counts["send"] += 1
        assert counts["send"] <= N_SEND
        return send_sems.at[counts["send"] - 1]

    def new_recv():
        counts["recv"] += 1
        assert counts["recv"] <= N_RECV
        return recv_sems.at[counts["recv"] - 1]

    def send(src, dst, s_sem, r_sem, device):
        pltpu.make_async_remote_copy(
            src_ref=src, dst_ref=dst, send_sem=s_sem, recv_sem=r_sem,
            device_id=device, device_id_type=MESH,
        ).start()

    def wait_recv(ref, r_sem):
        pltpu.make_async_remote_copy(
            src_ref=ref, dst_ref=ref, send_sem=send_sems.at[0], recv_sem=r_sem,
            device_id=sib, device_id_type=MESH,
        ).wait_recv()

    def drain(ref, s_sem):
        def step():
            pltpu.make_async_remote_copy(
                src_ref=ref, dst_ref=ref, send_sem=s_sem, recv_sem=recv_sems.at[0],
                device_id=sib, device_id_type=MESH,
            ).wait_send()

        drains.append(step)

    local = []

    def load(src, dst):
        copy = pltpu.make_async_copy(src, dst, local_sems.at[len(local)])
        copy.start()
        local.append(copy)
        return copy

    first = [
        load(tokens.at[pl.ds(0, 16)], tok.at[0, pl.ds(0, 16)]),
        load(tokens.at[pl.ds(16, 16)], tok.at[0, pl.ds(128, 16)]),
        load(sgate, wgu.at[pl.ds(pl.multiple_of(yo * 512, 512), 512), pl.ds(0, 128)]),
        load(sup, wgu.at[pl.ds(pl.multiple_of(yo * 512, 512), 512), pl.ds(128, 128)]),
        load(sdown, wd.at[yo]),
        load(ograd.at[pl.ds(0, 16)], dout.at[0, pl.ds(0, 16)]),
        load(ograd.at[pl.ds(16, 16)], dout.at[0, pl.ds(128, 16)]),
    ]
    later = [
        load(egate.at[0], wt.at[:, pl.ds(0, 128)]),
        load(eup.at[0], wt.at[:, pl.ds(128, 128)]),
        load(edown.at[0], wed),
    ]

    barrier = pltpu.get_barrier_semaphore()
    peers = [z_dev(d) for d in range(1, 8)] + [x_dev(d) for d in range(1, 4)] + [y_dev(1), y_dev(-1), sib]
    for device in peers:
        pl.semaphore_signal(barrier, inc=1, device_id=device, device_id_type=MESH)

    lane = lax.broadcasted_iota(jnp.int32, (16, 128), 1)
    lane_e = lax.rem(lane, 16)
    lane_half = lax.rem(lane // 16, 2)
    halves = []
    for half in range(2):
        total = jnp.zeros((16, 128), F32)
        for k in range(8):
            name = ids[half * 16 : half * 16 + 16, k : k + 1]
            weight = weights[half * 16 : half * 16 + 16, k : k + 1]
            total = total + jnp.where(lane_e == name, weight, 0.0)
        halves.append(total)
    value = jnp.where(lane_half == 0, halves[0], halves[1])
    high = value.astype(BF16).astype(F32)
    value = jnp.where(lane < 32, high, jnp.where(lane < 64, value - high, 0.0))
    coef[0, 0] = value.astype(BF16)

    pl.semaphore_wait(barrier, len(peers))
    for copy in first:
        copy.wait()

    def gather(buf, t0):
        s_z0, s_x0, s_b0 = new_send(), [new_send() for _ in range(3)], new_send()
        s_x1, s_z1, s_b1 = new_send(), new_send(), new_send()
        r_z0 = {(d, k): new_recv() for d in "RL" for k in range(1, 5)}
        r_x0 = {rel: new_recv() for rel in (1, 2, 3)}
        r_x1 = {rel: new_recv() for rel in (1, 2, 3)}
        r_z1 = {(d, k, c): new_recv() for d in "RL" for k in range(1, 5) for c in "ab"}
        r_b0, r_b1 = new_recv(), new_recv()
        step_dev = {"R": z_dev(1), "L": z_dev(-1)}

        def came(d, k):
            return (8 - k) % 8 if d == "R" else k % 8

        def z0_ref(d, k):
            rows = pl.ds(row_of(0, came(d, k)), 16)
            if k == 4:
                return buf.at[0, rows, pl.ds(0 if d == "R" else 512, 512)]
            return buf.at[0, rows]

        def z0_send(d, k):
            src = buf.at[0, pl.ds(row_of(0, came(d, k - 1)), 16)]
            if k == 4:
                src = buf.at[0, pl.ds(row_of(0, came(d, 3)), 16), pl.ds(0 if d == "R" else 512, 512)]
            send(src, z0_ref(d, k), s_z0, r_z0[d, k], step_dev[d])

        def x0_piece(r0, n):
            for i, d in enumerate((1, -1, 2)):
                send(
                    buf.at[0, pl.ds(r0, n)], buf.at[(-d) % 4, pl.ds(r0, n)], s_x0[i], r_x0[(-d) % 4], x_dev(d)
                )

        def z1_ref(z, c):
            rows = pl.ds(row_of(1, z), 16)
            return buf.at[pl.ds(0 if c == "a" else 2, 2), rows]

        def z1_send(d, k, c):
            send(z1_ref(came(d, k - 1), c), z1_ref(came(d, k), c), s_z1, r_z1[d, k, c], step_dev[d])

        def b0_send(rel):
            send(buf.at[rel, pl.ds(0, 128)], buf.at[rel, pl.ds(256, 128)], s_b0, r_b0, sib)

        def b1_send(z):
            send(
                buf.at[:, pl.ds(row_of(1, z), 16)], buf.at[:, pl.ds(row_of(1, z, 1), 16)], s_b1, r_b1, sib
            )

        def begin():
            own = pl.ds(128, 16)
            for d in (1, -1, 2):
                send(buf.at[0, own], buf.at[(-d) % 4, own], s_x1, r_x1[(-d) % 4], x_dev(d))
            for d in "RL":
                z0_send(d, 1)

        agenda.at(t0, begin)

        def z0_hop(k):
            for d in "RL":
                wait_recv(z0_ref(d, k), r_z0[d, k])
                if k < 4:
                    z0_send(d, k + 1)
            if k == 1:
                x0_piece(0, 48)
            if k == 2:
                x0_piece(48, 32)
            if k == 4:
                x0_piece(80, 48)
                b0_send(0)

        for k in range(1, 5):
            agenda.at(t0 + 2.7 * k, lambda k=k: z0_hop(k))

        def x0_done(rel):
            wait_recv(buf.at[rel, pl.ds(0, 128)], r_x0[rel])
            b0_send(rel)

        for i, rel in enumerate((1, 3, 2)):
            agenda.at(t0 + 15.5 + 0.4 * i, lambda rel=rel: x0_done(rel))

        def x1_done():
            own = pl.ds(128, 16)
            wait_recv(buf.at[1, own], r_x1[1])
            for d in "RL":
                z1_send(d, 1, "a")
            for rel in (2, 3):
                wait_recv(buf.at[rel, own], r_x1[rel])
            for d in "RL":
                z1_send(d, 1, "b")
            b1_send(0)

        agenda.at(t0 + 3.0, x1_done)

        def z1_hop(k, c):
            for d in "RL":
                if k == 4 and (d == "R") != (c == "a"):
                    continue
                z = came(d, k)
                wait_recv(z1_ref(z, c), r_z1[d, k, c])
                if k < 3 or (k == 3 and (d == "R") == (c == "a")):
                    z1_send(d, k + 1, c)
                if c == "b":
                    b1_send(z)

        for k in range(1, 5):
            agenda.at(t0 + 3.0 + 3.45 * k, lambda k=k: z1_hop(k, "a"))
            agenda.at(t0 + 4.4 + 3.45 * k, lambda k=k: z1_hop(k, "b"))

        def finish():
            wait_recv(buf.at[:, pl.ds(256, 128)], r_b0)
            wait_recv(buf.at[:, pl.ds(384, 128)], r_b1)

        done = t0 + 19.6
        agenda.at(done, finish)
        drain(buf.at[0, pl.ds(16, 112)], s_z0)
        for sem in s_x0:
            drain(buf.at[0, pl.ds(0, 128)], sem)
        drain(buf.at[:, pl.ds(0, 128)], s_b0)
        drain(buf.at[pl.ds(1, 3), pl.ds(128, 16)], s_x1)
        drain(buf.at[:, pl.ds(144, 112)], s_z1)
        drain(buf.at[:, pl.ds(128, 128)], s_b1)
        return done

    s_yw = [new_send() for _ in range(3)]
    r_yw = {(d, k, a): new_recv() for d in "RL" for k in range(1, 5) for a in range(3)}

    def yw_ref(a, origin, d, k):
        if a < 2:
            start, n = origin * 512, 512
            if k == 4:
                start, n = start + (0 if d == "R" else 256), 256
            return wgu.at[pl.ds(pl.multiple_of(start, 256), n), pl.ds(a * 128, 128)]
        if k == 4:
            return wd.at[origin, pl.ds(0 if d == "R" else 64, 64)]
        return wd.at[origin]

    def yw_origin(d, k):
        return lax.rem(yo + (8 - k if d == "R" else k), 8)

    def yw_send(d, k, a):
        ref = yw_ref(a, yw_origin(d, k - 1), d, k)
        send(ref, ref, s_yw[a], r_yw[d, k, a], y_dev(1 if d == "R" else -1))

    def yw_start():
        for a in range(3):
            for d in "RL":
                yw_send(d, 1, a)

    def yw_hop(k, a):
        for d in "RL":
            wait_recv(yw_ref(a, yw_origin(d, k), d, k), r_yw[d, k, a])
            if k < 4:
                yw_send(d, k + 1, a)

    agenda.at(0.0, yw_start)
    for k in range(1, 5):
        for a in range(3):
            when = 8.9 * (k - 1) + 2.95 * (a + 1) + 2.0 if k < 4 else 8.9 * 3 + 1.5 * (a + 1) + 2.0
            agenda.at(when, lambda k=k, a=a: yw_hop(k, a))
    drain(wgu.at[pl.ds(0, 3584), pl.ds(0, 128)], s_yw[0])
    drain(wgu.at[pl.ds(0, 3584), pl.ds(128, 128)], s_yw[1])
    drain(wd.at[pl.ds(0, 7)], s_yw[2])

    s_co, s_cb = new_send(), new_send()
    r_co = {z: new_recv() for z in range(1, 8)}
    r_cb = new_recv()

    def coef_start():
        for z in range(1, 8):
            send(coef.at[0, 0], coef.at[0, Z_POS[8 - z]], s_co, r_co[8 - z], z_dev(z))

    def coef_mirror():
        for z in range(1, 8):
            wait_recv(coef.at[0, Z_POS[z]], r_co[z])
        send(coef.at[0], coef.at[1], s_cb, r_cb, sib)

    agenda.at(4.0, coef_start)
    agenda.at(16.0, coef_mirror)
    drain(coef.at[0, pl.ds(0, 7)], s_co)
    drain(coef.at[0], s_cb)

    t_tok = gather(tok, 0.0)
    t_dout0 = 15.0
    t_dout = gather(dout, t_dout0)

    def weight_wait():
        for copy in later:
            copy.wait()

    agenda.at(t_tok + 0.01, weight_wait)
    s_hid = [new_send() for _ in range(2)]
    r_hid = {(d, i): new_recv() for d in (1, 2, 3) for i in range(2)}
    own_cols = pl.ds(pl.multiple_of(xo * 128, 128), 128)

    def project(buf, w, r0, n, out):
        out[pl.ds(r0, n), :] = jnp.dot(
            buf[0, pl.ds(r0, n), :],
            w[pl.ds(pl.multiple_of(xo * 1024, 1024), 1024), :],
            preferred_element_type=F32,
        )

        @pl.loop(1, 4)
        def _(rel):
            chunk = lax.rem(xo + rel, 4)
            out[pl.ds(r0, n), :] += jnp.dot(
                buf[rel, pl.ds(r0, n), :],
                w[pl.ds(pl.multiple_of(chunk * 1024, 1024), 1024), :],
                preferred_element_type=F32,
            )

    def teacher_hidden(i):
        r0 = 256 * (1 - i)
        project(tok, wt, r0, 256, gu)
        gate = gu[pl.ds(r0, 256), 0:128]
        up = gu[pl.ds(r0, 256), 128:256]
        hid[pl.ds(r0, 256), own_cols] = (gate * sigmoid(gate) * up).astype(BF16)
        ref = hid.at[pl.ds(r0, 256), own_cols]
        for d in (1, 3, 2):
            send(ref, ref, s_hid[i], r_hid[4 - d, i], x_dev(d))

    t_hid = t_tok + 0.02
    agenda.at(t_hid, lambda: teacher_hidden(0))
    agenda.at(t_hid + 1.2, lambda: teacher_hidden(1))
    for i in range(2):
        drain(hid.at[pl.ds(0, 256), pl.ds(0, 384)], s_hid[i])

    s_sp = new_send()
    r_sp = new_recv()
    s_rs = new_send()
    r_rs = {z: new_recv() for z in range(1, 8)}

    def coef_column(other, half):
        lanes = lax.broadcasted_iota(jnp.int32, (128, 128), 1)
        rows = coef[other].astype(F32).reshape(128, 128)
        wanted = (lanes == half * 16 + eo) | (lanes == 32 + half * 16 + eo)
        return jnp.sum(jnp.where(wanted, rows, 0.0), axis=1, keepdims=True)

    def teacher_down(i):
        other = 1 - i
        r0 = 256 * other
        for d in (1, 3, 2):
            cols = pl.ds(pl.multiple_of(lax.rem(xo + d, 4) * 128, 128), 128)
            wait_recv(hid.at[pl.ds(r0, 256), cols], r_hid[d, i])
        if i == 0:
            wait_recv(coef.at[1], r_cb)
        if i == 1:
            wait_recv(sibp, r_sp)
        for half in range(2):
            scale = coef_column(other, half)
            for q in range(2):
                cols = slice(q * 512, q * 512 + 512)
                res = jnp.dot(
                    hid[pl.ds(r0 + half * 128, 128), :], wed[:, cols], preferred_element_type=F32
                )
                res = res * scale
                if i == 1:
                    res = res + sibp[half, :, cols].astype(F32)
                part[other, half, :, cols] = res.astype(BF16)
        if i == 0:
            send(part.at[1], sibp, s_sp, r_sp, sib)
        else:
            for z in (4, 3, 5, 2, 6, 1, 7):
                rows = pl.ds(Z_POS[z] * 16, 16)
                send(part.at[0, :, rows], rsb.at[8 - z], s_rs, r_rs[8 - z], z_dev(z))

    t_down = t_hid + 6.0
    agenda.at(t_down, lambda: teacher_down(0))
    agenda.at(t_down + 3.5, lambda: teacher_down(1))
    drain(part.at[1], s_sp)
    drain(part.at[0, :, pl.ds(16, 112)], s_rs)

    def teacher_sum():
        for z in range(1, 8):
            wait_recv(rsb.at[z], r_rs[z])
        for half in range(2):
            total = part[0, half, 0:16, :].astype(F32)
            for z in range(1, 8):
                total = total + rsb[z, half].astype(F32)
            row = total.astype(BF16)
            t_out[half * 16 : half * 16 + 16, :] = row
            act[0, half * 128 : half * 128 + 16, :] = row

    t_sum = t_down + 3.5 + 14.0
    agenda.at(t_sum, teacher_sum)

    def student_back():
        hg[...] = jnp.zeros_like(hg)

        @pl.loop(0, 4)
        def _(rel):
            chunk = lax.rem(xo + rel, 4)
            for j in range(2):
                hg[...] += lax.dot_general(
                    dout[rel, :, j * 512 : j * 512 + 512],
                    wd[chunk * 2 + j],
                    (((1,), (1,)), ((), ())),
                    preferred_element_type=F32,
                )

    agenda.at(max(t_dout + 0.1, 35.5), student_back)
    t_act = gather(act, t_sum + 0.1)

    def student_rows(i):
        r0 = 256 * i
        project(act, wgu, r0, 256, gu)
        gate = gu[pl.ds(r0, 256), 0:128]
        up = gu[pl.ds(r0, 256), 128:256]
        back = hg[pl.ds(r0, 256), :]
        sig = sigmoid(gate)
        silu = gate * sig
        cols = slice(r0, r0 + 256)
        gt[0:128, cols] = (back * up * (sig * (1.0 + gate * (1.0 - sig)))).T.astype(BF16)
        gt[128:256, cols] = (back * silu).T.astype(BF16)
        gt[256:384, cols] = (silu * up).T.astype(BF16)

    agenda.at(t_act + 0.1, lambda: student_rows(0))
    agenda.at(t_act + 0.2, lambda: student_rows(1))

    s_yg = [new_send() for _ in range(3)]
    r_yg = {(d, k, a): new_recv() for d in "RL" for k in range(4) for a in range(3)}

    def term(k, a):
        owner = lax.rem(yo + k, 8)
        rel = lax.rem(owner // 2 - xo + 4, 4)
        cols = pl.ds(pl.multiple_of(lax.rem(owner, 2) * 512, 512), 512)
        if a == 0:
            grad[k, 0:256, :] = jnp.dot(
                gt[0:256, :], act[rel, :, cols], preferred_element_type=F32
            ).astype(BF16)
        else:
            grad[k, 256:384, :] = jnp.dot(
                gt[256:384, :], dout[rel, :, cols], preferred_element_type=F32
            ).astype(BF16)

    def yg_ref(d, k, a):
        if k == 0:
            return ring.at[0 if d == "R" else 1, 0, a, pl.ds(0 if d == "R" else 64, 64)]
        return ring.at[0 if d == "R" else 1, k, a]

    def yg_send(d, k, a):
        if k == 0:
            src = grad.at[4, pl.ds(a * 128 + (0 if d == "R" else 64), 64)]
        else:
            src = grad.at[4 - k if d == "R" else 4 + k, pl.ds(a * 128, 128)]
        send(src, yg_ref(d, k, a), s_yg[a], r_yg[d, k, a], y_dev(1 if d == "R" else -1))

    t_g = t_act + 1.0

    def first_terms():
        term(4, 0)
        for a in range(2):
            for d in "RL":
                yg_send(d, 0, a)
        term(4, 1)
        for d in "RL":
            yg_send(d, 0, 2)
        for k in (3, 5):
            for a in range(2):
                term(k, a)

    agenda.at(t_g, first_terms)
    for i, k in enumerate((2, 6, 1, 7, 0)):
        for a in range(2):
            agenda.at(t_g + 8.0 + 3.2 * i + 1.5 * a, lambda k=k, a=a: term(k, a))

    def yg_hop(k, a):
        for d in "RL":
            wait_recv(yg_ref(d, k - 1, a), r_yg[d, k - 1, a])
            way = 0 if d == "R" else 1
            mine = 4 - k if d == "R" else 4 + k
            lo, n = a * 128, 128
            off = 0
            if k == 1:
                off, n = (0, 64) if d == "R" else (64, 64)
            grad[mine, lo + off : lo + off + n, :] = (
                grad[mine, lo + off : lo + off + n, :].astype(F32)
                + ring[way, k - 1, a, off : off + n, :].astype(F32)
            ).astype(BF16)
            yg_send(d, k, a)

    for k in range(1, 4):
        for a in range(3):
            agenda.at(t_g + 3.0 + 8.9 * (k - 1) + 2.95 * a, lambda k=k, a=a: yg_hop(k, a))

    def yg_last(a):
        for d in "RL":
            wait_recv(yg_ref(d, 3, a), r_yg[d, 3, a])
        total = (
            grad[0, a * 128 : a * 128 + 128, :].astype(F32)
            + ring[0, 3, a].astype(F32)
            + ring[1, 3, a].astype(F32)
        )
        if a == 0:
            gg_out[...] = total.T
        elif a == 1:
            gu_out[...] = total.T
        else:
            gd_out[...] = total

    for a in range(3):
        agenda.at(t_g + 3.0 + 8.9 * 3 + 2.95 * a, lambda a=a: yg_last(a))
        drain(grad.at[pl.ds(1, 7), pl.ds(a * 128, 128)], s_yg[a])

    agenda.run()
    for step in drains:
        step()


def body(*args):
    any_spec = pl.BlockSpec(memory_space=pl.ANY)
    vmem = pl.BlockSpec(memory_space=pltpu.VMEM)
    scratch = [
        pltpu.VMEM((4, 512, 1024), BF16),
        pltpu.VMEM((4, 512, 1024), BF16),
        pltpu.VMEM((4, 512, 1024), BF16),
        pltpu.VMEM((4096, 256), BF16),
        pltpu.VMEM((512, 1024), BF16),
        pltpu.VMEM((4096, 256), BF16),
        pltpu.VMEM((8, 128, 512), BF16),
        pltpu.VMEM((512, 512), BF16),
        pltpu.VMEM((2, 8, 16, 128), BF16),
        pltpu.VMEM((2, 2, 128, 1024), BF16),
        pltpu.VMEM((2, 128, 1024), BF16),
        pltpu.VMEM((8, 2, 16, 1024), BF16),
        pltpu.VMEM((512, 256), F32),
        pltpu.VMEM((512, 128), F32),
        pltpu.VMEM((384, 512), BF16),
        pltpu.VMEM((8, 384, 512), BF16),
        pltpu.VMEM((2, 4, 3, 128, 512), BF16),
        pltpu.SemaphoreType.DMA((N_SEND,)),
        pltpu.SemaphoreType.DMA((N_RECV,)),
        pltpu.SemaphoreType.DMA((10,)),
    ]
    return pl.pallas_call(
        kernel,
        out_shape=(
            jax.ShapeDtypeStruct((32, 1024), BF16),
            jax.ShapeDtypeStruct((512, 128), F32),
            jax.ShapeDtypeStruct((512, 128), F32),
            jax.ShapeDtypeStruct((128, 512), F32),
        ),
        in_specs=[any_spec, vmem, vmem] + [any_spec] * 7,
        out_specs=(vmem,) * 4,
        scratch_shapes=scratch,
        compiler_params=pltpu.CompilerParams(
            collective_id=1, has_side_effects=True, vmem_limit_bytes=52 * 1024 * 1024
        ),
        cost_estimate=pl.CostEstimate(flops=5_000_000_000, bytes_accessed=12_000_000, transcendentals=400_000),
        name="distill_window",
    )(*args)


def solution(mesh):
    in_specs = (
        P(("seq", "exp"), "tp"),
        P(("seq", "exp"), None),
        P(("seq", "exp"), None),
        P("exp", None, "tp"),
        P("exp", None, "tp"),
        P("exp", None, "tp"),
        P("seq", ("exp", "tp")),
        P("seq", ("exp", "tp")),
        P(("exp", "tp"), "seq"),
        P(("seq", "exp"), "tp"),
    )
    out_specs = (
        P(("seq", "exp"), "tp"),
        P("seq", ("exp", "tp")),
        P("seq", ("exp", "tp")),
        P(("exp", "tp"), "seq"),
    )
    return jax.shard_map(body, mesh=mesh, in_specs=in_specs, out_specs=out_specs, check_vma=False)
```

```python
import jax
import jax.numpy as jnp
from jax import lax
from jax.experimental import pallas as pl
from jax.experimental.pallas import tpu as pltpu
from jax.sharding import PartitionSpec as P

MESH = pl.DeviceIdType.MESH
F32 = jnp.float32
BF16 = jnp.bfloat16
Z_ORDER = (0, 1, 7, 2, 6, 3, 5, 4)
Z_POS = {z: i for i, z in enumerate(Z_ORDER)}
N_RECV = 400
N_SEND = 96


WAVES = ((0, 160), (320, 96))
Z_FIRST = 640


def row_at(pos, other=0):
    return other * 160 + pos * 32 if pos < 5 else 320 + other * 96 + (pos - 5) * 32


def row_of(z, other=0):
    return row_at(Z_POS[z % 8], other)


def sigmoid(a):
    return 1.0 / (1.0 + jnp.exp(-a))


class Agenda:
    def __init__(self):
        self.steps = []

    def at(self, time, step):
        self.steps.append((time, len(self.steps), step))

    def run(self):
        for _, _, step in sorted(self.steps, key=lambda s: (s[0], s[1])):
            step()


def kernel(
    tokens, ids, weights, egate, eup, edown, sgate, sup, sdown, ograd,
    t_hbm, gg_hbm, gu_hbm, gd_hbm,
    tok, act, dout, wt, wed, wgu, wd, hid, coef, part, sibp, rsb, gu, hg, gt, grad, ring, t_out, gg_out, gu_out, gd_out,
    send_sems, recv_sems, local_sems,
):
    yo = lax.axis_index("seq")
    eo = lax.axis_index("exp")
    xo = lax.axis_index("tp")
    zo = eo // 2
    co = lax.rem(eo, 2)

    def z_dev(d):
        return (yo, lax.rem(zo + d + 8, 8) * 2 + co, xo)

    def x_dev(d):
        return (yo, eo, lax.rem(xo + d + 4, 4))

    def y_dev(d):
        return (lax.rem(yo + d + 8, 8), eo, xo)

    sib = (yo, zo * 2 + (1 - co), xo)
    agenda = Agenda()
    drains = []
    counts = {"send": 0, "recv": 0, "local": 0}

    def new_send():
        counts["send"] += 1
        assert counts["send"] <= N_SEND
        return send_sems.at[counts["send"] - 1]

    def new_recv():
        counts["recv"] += 1
        assert counts["recv"] <= N_RECV
        return recv_sems.at[counts["recv"] - 1]

    def send(src, dst, s_sem, r_sem, device):
        pltpu.make_async_remote_copy(
            src_ref=src, dst_ref=dst, send_sem=s_sem, recv_sem=r_sem,
            device_id=device, device_id_type=MESH,
        ).start()

    def wait_recv(ref, r_sem):
        pltpu.make_async_remote_copy(
            src_ref=ref, dst_ref=ref, send_sem=send_sems.at[0], recv_sem=r_sem,
            device_id=sib, device_id_type=MESH,
        ).wait_recv()

    def drain(ref, s_sem):
        def step():
            pltpu.make_async_remote_copy(
                src_ref=ref, dst_ref=ref, send_sem=s_sem, recv_sem=recv_sems.at[0],
                device_id=sib, device_id_type=MESH,
            ).wait_send()

        drains.append(step)

    local = []

    def load(src, dst):
        copy = pltpu.make_async_copy(src, dst, local_sems.at[len(local)])
        copy.start()
        local.append(copy)
        return copy

    first = [
        load(tokens, tok.at[0, pl.ds(0, 32)]),
        load(sgate, wgu.at[pl.ds(pl.multiple_of(yo * 512, 512), 512), pl.ds(0, 128)]),
        load(sup, wgu.at[pl.ds(pl.multiple_of(yo * 512, 512), 512), pl.ds(128, 128)]),
        load(sdown, wd.at[yo]),
        load(ograd, dout.at[0, pl.ds(0, 32)]),
    ]
    stores = []

    def store(i, src, dst):
        copy = pltpu.make_async_copy(src, dst, local_sems.at[8 + i])
        copy.start()
        stores.append(copy)

    later = [
        load(egate.at[0], wt.at[:, pl.ds(0, 128)]),
        load(eup.at[0], wt.at[:, pl.ds(128, 128)]),
        load(edown.at[0], wed),
    ]

    barrier = pltpu.get_barrier_semaphore()
    peers = [z_dev(d) for d in range(1, 8)] + [x_dev(d) for d in range(1, 4)] + [y_dev(1), y_dev(-1), sib]
    for device in peers:
        pl.semaphore_signal(barrier, inc=1, device_id=device, device_id_type=MESH)

    lane = lax.broadcasted_iota(jnp.int32, (16, 128), 1)
    lane_e = lax.rem(lane, 16)
    lane_half = lax.rem(lane // 16, 2)
    blank = jnp.zeros((8, 96), jnp.int32)
    names = jnp.concatenate([ids[...], blank], axis=1).T
    shares = jnp.concatenate([weights[...], blank.astype(F32)], axis=1).T
    halves = []
    for half in range(2):
        total = jnp.zeros((16, 128), F32)
        for k in range(8):
            name = names[half * 16 : half * 16 + 16, k : k + 1]
            weight = shares[half * 16 : half * 16 + 16, k : k + 1]
            total = total + jnp.where(lane_e == name, weight, 0.0)
        halves.append(total)
    value = jnp.where(lane_half == 0, halves[0], halves[1])
    high = value.astype(BF16).astype(F32)
    value = jnp.where(lane < 32, high, jnp.where(lane < 64, value - high, 0.0))
    coef[0, 0] = value.astype(BF16)

    pl.semaphore_wait(barrier, len(peers))
    for copy in first:
        copy.wait()

    def gather(buf, t0, times=None):
        s_z0, s_x0, s_f0, s_b0 = new_send(), [new_send() for _ in range(2)], new_send(), new_send()
        s_x2, s_x1, s_z1, s_b1 = new_send(), new_send(), new_send(), new_send()
        pieces = ((0, 1), (1, 2), (3, 2), (5, 2), (7, 1))
        r_z0 = {(d, k): new_recv() for d in "RL" for k in range(1, 5)}
        r_x0 = {(rel, k): new_recv() for rel in (1, 3) for k in range(5)}
        r_f0 = {(rel, k): new_recv() for rel in (1, 3) for k in range(4)}
        r_x2 = new_recv()
        r_x1 = {rel: new_recv() for rel in (1, 2, 3)}
        r_z1 = {(d, k, c): new_recv() for d in "RL" for k in range(1, 5) for c in range(4)}
        r_b0, r_b1 = [new_recv() for _ in range(2)], [new_recv() for _ in range(2)]
        step_dev = {"R": z_dev(1), "L": z_dev(-1)}
        cols0, cols1 = pl.ds(0, Z_FIRST), pl.ds(Z_FIRST, 1024 - Z_FIRST)
        part_cols = {"R": pl.ds(0, 384), "L": pl.ds(384, Z_FIRST - 384)}

        def came(d, k):
            return (8 - k) % 8 if d == "R" else k % 8

        def z0_ref(z, d, k):
            return buf.at[0, pl.ds(row_of(z), 32), part_cols[d] if k == 4 else cols0]

        def z0_send(d, k):
            send(z0_ref(came(d, k - 1), d, k), z0_ref(came(d, k), d, k), s_z0, r_z0[d, k], step_dev[d])

        def piece_ref(rel, k, cols=cols0, other=0):
            pos, n = pieces[k]
            return buf.at[rel, pl.ds(row_at(pos, other), 32 * n), cols]

        def x0_piece(k):
            for i, d in enumerate((1, -1)):
                send(piece_ref(0, k), piece_ref((-d) % 4, k), s_x0[i], r_x0[(-d) % 4, k], x_dev(d))
            if k == 4:
                send(piece_ref(0, k), piece_ref(2, k), s_x2, r_x2, x_dev(2))

        def z1_ref(z, c):
            return buf.at[c, pl.ds(row_of(z), 32), cols1]

        def z1_send(d, k, c):
            send(z1_ref(came(d, k - 1), c), z1_ref(came(d, k), c), s_z1, r_z1[d, k, c], step_dev[d])

        def b0_send(rel, k):
            send(piece_ref(rel, k), piece_ref(rel, k, other=1), s_b0, r_b0[0 if k < 3 else 1], sib)

        def b1_send(z):
            send(
                buf.at[:, pl.ds(row_of(z), 32), cols1],
                buf.at[:, pl.ds(row_of(z, 1), 32), cols1],
                s_b1, r_b1[0 if Z_POS[z] < 5 else 1], sib,
            )

        plan = {("begin",): 0.0, ("ready", 0): 13.5, ("ready", 1): 16.6}
        for k, (there, beyond) in enumerate(((3.1, 11.0), (6.8, 11.5), (9.8, 12.3), (12.7, 15.4), (14.6, 15.5))):
            plan["x0", k] = 2.9 * k + 0.01
            plan["x0_done", k], plan["f0_done", k] = there, beyond
        plan["x1",] = 2.95
        for k in range(1, 5):
            plan["z0", k] = 2.9 * k
            for c, when in ((0, 0.2), (1, 2.5), (3, 3.0), (2, 3.5)):
                plan["z1", k, c] = 2.9 * k + when
        plan.update(times or {})

        def at(name, step):
            agenda.at(t0 + plan[name], step)

        def begin():
            for d in "RL":
                z0_send(d, 1)
            for d in (1, -1, 2):
                send(z1_ref(0, 0), z1_ref(0, (-d) % 4), s_x1, r_x1[(-d) % 4], x_dev(d))
            for d in "RL":
                z1_send(d, 1, 0)

        at(("begin",), begin)

        def z0_hop(k):
            for d in "RL":
                wait_recv(z0_ref(came(d, k), d, k), r_z0[d, k])
                if k < 4:
                    z0_send(d, k + 1)

        def x0_start(k):
            x0_piece(k)
            b0_send(0, k)

        for k in range(1, 5):
            at(("z0", k), lambda k=k: z0_hop(k))
        for k in range(5):
            at(("x0", k), lambda k=k: x0_start(k))

        def x0_done(rel, k):
            wait_recv(piece_ref(rel, k), r_x0[rel, k])
            if k < 4:
                d, way = (1, "R") if rel == 3 else (-1, "L")
                send(
                    piece_ref(rel, k, part_cols[way]), piece_ref(2, k, part_cols[way]),
                    s_f0, r_f0[rel, k], x_dev(d),
                )
            b0_send(rel, k)

        def f0_done(k):
            if k == 4:
                wait_recv(piece_ref(2, k), r_x2)
            else:
                for rel, way in ((3, "R"), (1, "L")):
                    wait_recv(piece_ref(2, k, part_cols[way]), r_f0[rel, k])
            b0_send(2, k)

        for k in range(5):
            for rel in (1, 3):
                at(("x0_done", k), lambda rel=rel, k=k: x0_done(rel, k))
            at(("f0_done", k), lambda k=k: f0_done(k))

        def x1_done(rel):
            wait_recv(z1_ref(0, rel), r_x1[rel])
            for d in "RL":
                z1_send(d, 1, rel)
            if rel == 2:
                b1_send(0)

        for rel in (1, 3, 2):
            at(("x1",), lambda rel=rel: x1_done(rel))

        def z1_hop(k, c):
            for d in "RL":
                if k == 4 and (d == "R") != (c in (0, 1)):
                    continue
                z = came(d, k)
                wait_recv(z1_ref(z, c), r_z1[d, k, c])
                if k < 3 or (k == 3 and (d == "R") == (c in (0, 1))):
                    z1_send(d, k + 1, c)
                if c == 2:
                    b1_send(z)

        for k in range(1, 5):
            for c in (0, 1, 3, 2):
                at(("z1", k, c), lambda k=k, c=c: z1_hop(k, c))

        def finish(wave):
            first, n = WAVES[wave]
            rows = pl.ds(first + n, n)
            wait_recv(buf.at[:, rows, cols0], r_b0[wave])
            wait_recv(buf.at[:, rows, cols1], r_b1[wave])

        for wave in range(2):
            at(("ready", wave), lambda wave=wave: finish(wave))
        drain(buf.at[0, pl.ds(0, 224), cols0], s_z0)
        for sem in s_x0:
            drain(buf.at[0, pl.ds(0, 256), cols0], sem)
        drain(buf.at[0, pl.ds(0, 224), cols0], s_f0)
        drain(buf.at[0, pl.ds(0, 32), cols0], s_x2)
        drain(buf.at[:, pl.ds(0, 256), cols0], s_b0)
        drain(buf.at[pl.ds(1, 3), pl.ds(0, 32), cols1], s_x1)
        drain(buf.at[:, pl.ds(0, 224), cols1], s_z1)
        drain(buf.at[:, pl.ds(0, 256), cols1], s_b1)
        return [t0 + plan["ready", 0], t0 + plan["ready", 1]]

    s_yw = [new_send() for _ in range(3)]
    r_yw = {(d, k, a): new_recv() for d in "RL" for k in range(1, 5) for a in range(3)}

    def yw_ref(a, origin, d, k):
        if a < 2:
            start, n = origin * 512, 512
            if k == 4:
                start, n = start + (0 if d == "R" else 256), 256
            return wgu.at[pl.ds(pl.multiple_of(start, 256), n), pl.ds(a * 128, 128)]
        if k == 4:
            return wd.at[origin, pl.ds(0 if d == "R" else 64, 64)]
        return wd.at[origin]

    def yw_origin(d, k):
        return lax.rem(yo + (8 - k if d == "R" else k), 8)

    def yw_send(d, k, a):
        ref = yw_ref(a, yw_origin(d, k - 1), d, k)
        send(ref, ref, s_yw[a], r_yw[d, k, a], y_dev(1 if d == "R" else -1))

    def yw_start():
        for a in range(3):
            for d in "RL":
                yw_send(d, 1, a)

    def yw_hop(k, a):
        for d in "RL":
            wait_recv(yw_ref(a, yw_origin(d, k), d, k), r_yw[d, k, a])
            if k < 4:
                yw_send(d, k + 1, a)

    agenda.at(0.01, yw_start)
    for k in range(1, 5):
        for a in range(3):
            when = 8.9 * (k - 1) + 2.95 * (a + 1) + 2.0 if k < 4 else 8.9 * 3 + 1.5 * (a + 1) + 2.0
            agenda.at(1.25 * when + 2.0, lambda k=k, a=a: yw_hop(k, a))
    drain(wgu.at[pl.ds(0, 3584), pl.ds(0, 128)], s_yw[0])
    drain(wgu.at[pl.ds(0, 3584), pl.ds(128, 128)], s_yw[1])
    drain(wd.at[pl.ds(0, 7)], s_yw[2])

    s_co, s_cb = new_send(), new_send()
    r_co = {z: new_recv() for z in range(1, 8)}
    r_cb = new_recv()

    def coef_start():
        for z in range(1, 8):
            send(coef.at[0, 0], coef.at[0, Z_POS[8 - z]], s_co, r_co[8 - z], z_dev(z))

    def coef_mirror():
        for z in range(1, 8):
            wait_recv(coef.at[0, Z_POS[z]], r_co[z])
        send(coef.at[0], coef.at[1], s_cb, r_cb, sib)

    agenda.at(4.0, coef_start)
    agenda.at(16.0, coef_mirror)
    drain(coef.at[0, pl.ds(0, 7)], s_co)
    drain(coef.at[0], s_cb)

    t_tok = gather(tok, 0.0)
    late = {("begin",): 11.0, ("x1",): 15.1, ("ready", 0): 31.0, ("ready", 1): 32.0}
    for k, (when, start, there, beyond) in enumerate(
        ((0, 18.3, 22.5, 27.0), (15.2, 18.4, 24.2, 28.0), (18.2, 20.7, 25.9, 29.0), (20.6, 22.6, 26.5, 30.0), (26.0, 26.1, 30.0, 30.1))
    ):
        late["x0", k], late["x0_done", k], late["f0_done", k] = start, there, beyond
        if k:
            late["z0", k] = when
            for c in range(4):
                late["z1", k, c] = when + (0.1 if k < 3 else 2.0 if k == 3 else 0.4)
    gather(dout, 0.0, late)

    def weight_wait():
        for copy in later:
            copy.wait()

    agenda.at(t_tok[0] + 0.01, weight_wait)
    s_hid = [new_send() for _ in range(2)]
    r_hid = {(d, w): new_recv() for d in (1, 2, 3) for w in range(2)}

    def hid_cols(d):
        return pl.ds(pl.multiple_of(lax.rem(xo + d, 4) * 128, 128), 128)

    def project(buf, w, rows, out):
        out[rows, :] = jnp.dot(
            buf[0, rows, :],
            w[pl.ds(pl.multiple_of(xo * 1024, 1024), 1024), :],
            preferred_element_type=F32,
        )

        @pl.loop(1, 4)
        def _(rel):
            chunk = lax.rem(xo + rel, 4)
            out[rows, :] += jnp.dot(
                buf[rel, rows, :],
                w[pl.ds(pl.multiple_of(chunk * 1024, 1024), 1024), :],
                preferred_element_type=F32,
            )

    def wave_rows(wave):
        first, n = WAVES[wave]
        return pl.ds(first, 2 * n)

    def teacher_hidden(wave):
        rows = wave_rows(wave)
        project(tok, wt, rows, gu)
        gate = gu[rows, 0:128]
        up = gu[rows, 128:256]
        hid[rows, hid_cols(0)] = (gate * sigmoid(gate) * up).astype(BF16)
        ref = hid.at[rows, hid_cols(0)]
        for d in (1, 3, 2):
            send(ref, ref, s_hid[wave], r_hid[4 - d, wave], x_dev(d))

    for wave in range(2):
        agenda.at(t_tok[wave] + 0.02, lambda wave=wave: teacher_hidden(wave))
        drain(hid.at[wave_rows(wave), pl.ds(0, 384)], s_hid[wave])

    s_sp = [new_send() for _ in range(2)]
    r_sp = [new_recv() for _ in range(2)]
    s_rs = new_send()
    r_rs = {z: new_recv() for z in range(1, 8)}

    def coef_column(other, wave):
        start, n = ((0, 5), (5, 3))[wave]
        lanes = lax.broadcasted_iota(jnp.int32, (n, 16, 128), 2)
        rows = coef[other, start : start + n].astype(F32)
        cols = []
        for half in range(2):
            wanted = (lanes == half * 16 + eo) | (lanes == 32 + half * 16 + eo)
            cols.append(jnp.sum(jnp.where(wanted, rows, 0.0), axis=2, keepdims=True))
        return jnp.concatenate(cols, axis=1).reshape(n * 32, 1)

    def hid_wait(wave):
        for d in (1, 3, 2):
            wait_recv(hid.at[wave_rows(wave), hid_cols(d)], r_hid[d, wave])
        if wave == 0:
            wait_recv(coef.at[1], r_cb)

    def teacher_down(wave, other):
        first, n = WAVES[wave]
        rows = pl.ds(first + other * n, n)
        own = pl.ds(first, n)
        scale = coef_column(other, wave)
        if other == 0:
            wait_recv(sibp.at[own], r_sp[wave])
        for q in range(2):
            cols = slice(q * 512, q * 512 + 512)
            res = jnp.dot(hid[rows, :], wed[:, cols], preferred_element_type=F32) * scale
            if other == 0:
                res = res + sibp[own, cols].astype(F32)
            part[rows, cols] = res.astype(BF16)
        if other == 1:
            send(part.at[rows], sibp.at[own], s_sp[wave], r_sp[wave], sib)
        else:
            for z in ((2, 6, 1, 7), (4, 3, 5))[wave]:
                send(part.at[pl.ds(row_of(z), 32)], rsb.at[8 - z], s_rs, r_rs[8 - z], z_dev(z))

    t_down = [20.2, 22.9]
    for wave in range(2):
        agenda.at(t_down[wave], lambda wave=wave: hid_wait(wave))
        for other in (1, 0):
            agenda.at(
                t_down[wave] + (0.1, 2.1)[1 - other],
                lambda wave=wave, other=other: teacher_down(wave, other),
            )
        first, n = WAVES[wave]
        drain(part.at[pl.ds(first + n, n)], s_sp[wave])
    drain(part.at[pl.ds(0, 224)], s_rs)

    def teacher_sum():
        total = part[0:32, :].astype(F32)
        for z in (1, 7, 2, 6, 3, 5, 4):
            wait_recv(rsb.at[z], r_rs[z])
        for z in range(1, 8):
            total = total + rsb[z].astype(F32)
        row = total.astype(BF16)
        t_out[...] = row
        store(0, t_out, t_hbm)
        act[0, 0:32, :] = row

    t_sum = 35.0
    agenda.at(t_sum, teacher_sum)

    def student_back(rel):
        chunk = lax.rem(xo + rel, 4)
        total = jnp.zeros((512, 128), F32) if rel == 0 else hg[...]
        for j in range(2):
            total = total + lax.dot_general(
                dout[rel, :, j * 512 : j * 512 + 512],
                wd[chunk * 2 + j],
                (((1,), (1,)), ((), ())),
                preferred_element_type=F32,
            )
        hg[...] = total

    t_act = gather(act, t_sum + 0.1)
    for rel, when in enumerate((1.0, 4.0, 7.0, 10.0)):
        agenda.at(max(45.5, t_sum + 0.1 + when), lambda rel=rel: student_back(rel))

    def student_rows(wave):
        first, n = WAVES[wave]
        rows = pl.ds(first, 2 * n)
        project(act, wgu, rows, gu)
        gate = gu[rows, 0:128]
        up = gu[rows, 128:256]
        back = hg[rows, :]
        sig = sigmoid(gate)
        silu = gate * sig
        terms = (back * up * (sig * (1.0 + gate * (1.0 - sig))), back * silu, silu * up)
        for i, term in enumerate(terms):
            gt[i * 128 : i * 128 + 128, rows] = term.T.astype(BF16)

    for wave in range(2):
        agenda.at(t_act[wave] + 0.1, lambda wave=wave: student_rows(wave))

    s_yg = [new_send() for _ in range(3)]
    r_yg = {(d, k, a): new_recv() for d in "RL" for k in range(4) for a in range(3)}

    def term(k, a):
        owner = lax.rem(yo + k, 8)
        rel = lax.rem(owner // 2 - xo + 4, 4)
        cols = pl.ds(pl.multiple_of(lax.rem(owner, 2) * 512, 512), 512)
        if a == 0:
            grad[k, 0:256, :] = jnp.dot(
                gt[0:256, :], act[rel, :, cols], preferred_element_type=F32
            ).astype(BF16)
        else:
            grad[k, 256:384, :] = jnp.dot(
                gt[256:384, :], dout[rel, :, cols], preferred_element_type=F32
            ).astype(BF16)

    def yg_ref(d, k, a):
        if k == 0:
            return ring.at[0 if d == "R" else 1, 0, a, pl.ds(0 if d == "R" else 64, 64)]
        return ring.at[0 if d == "R" else 1, k, a]

    def yg_send(d, k, a):
        if k == 0:
            src = grad.at[4, pl.ds(a * 128 + (0 if d == "R" else 64), 64)]
        else:
            src = grad.at[4 - k if d == "R" else 4 + k, pl.ds(a * 128, 128)]
        send(src, yg_ref(d, k, a), s_yg[a], r_yg[d, k, a], y_dev(1 if d == "R" else -1))

    t_g = t_act[1] + 1.0

    def first_terms():
        term(4, 0)
        for a in range(2):
            for d in "RL":
                yg_send(d, 0, a)
        term(4, 1)
        for d in "RL":
            yg_send(d, 0, 2)
        for k in (3, 5):
            for a in range(2):
                term(k, a)

    agenda.at(t_g, first_terms)
    for i, k in enumerate((2, 6, 1, 7, 0)):
        for a in range(2):
            agenda.at(t_g + 8.0 + 3.2 * i + 1.5 * a, lambda k=k, a=a: term(k, a))

    def yg_hop(k, a):
        for d in "RL":
            wait_recv(yg_ref(d, k - 1, a), r_yg[d, k - 1, a])
            way = 0 if d == "R" else 1
            mine = 4 - k if d == "R" else 4 + k
            lo, n = a * 128, 128
            off = 0
            if k == 1:
                off, n = (0, 64) if d == "R" else (64, 64)
            grad[mine, lo + off : lo + off + n, :] = (
                grad[mine, lo + off : lo + off + n, :].astype(F32)
                + ring[way, k - 1, a, off : off + n, :].astype(F32)
            ).astype(BF16)
            yg_send(d, k, a)

    for k in range(1, 4):
        for a in range(3):
            agenda.at(t_g + 3.0 + 8.9 * (k - 1) + 2.95 * a, lambda k=k, a=a: yg_hop(k, a))

    def yg_last(a):
        for d in "RL":
            wait_recv(yg_ref(d, 3, a), r_yg[d, 3, a])
        total = (
            grad[0, a * 128 : a * 128 + 128, :].astype(F32)
            + ring[0, 3, a].astype(F32)
            + ring[1, 3, a].astype(F32)
        )
        if a == 0:
            gg_out[...] = total.T
            store(1, gg_out, gg_hbm)
        elif a == 1:
            gu_out[...] = total.T
            store(2, gu_out, gu_hbm)
        else:
            gd_out[...] = total
            store(3, gd_out, gd_hbm)

    for a in range(3):
        agenda.at(t_g + 3.0 + 8.9 * 3 + 2.95 * a, lambda a=a: yg_last(a))
        drain(grad.at[pl.ds(1, 7), pl.ds(a * 128, 128)], s_yg[a])

    agenda.run()
    for step in drains:
        step()
    for copy in stores:
        copy.wait()


def hand_over(*refs):
    for src, dst in zip(refs[:4], refs[4:]):
        dst[...] = src[...]


def body(*args):
    any_spec = pl.BlockSpec(memory_space=pl.ANY)
    vmem = pl.BlockSpec(memory_space=pltpu.VMEM)
    scratch = [
        pltpu.VMEM((4, 512, 1024), BF16),
        pltpu.VMEM((4, 512, 1024), BF16),
        pltpu.VMEM((4, 512, 1024), BF16),
        pltpu.VMEM((4096, 256), BF16),
        pltpu.VMEM((512, 1024), BF16),
        pltpu.VMEM((4096, 256), BF16),
        pltpu.VMEM((8, 128, 512), BF16),
        pltpu.VMEM((512, 512), BF16),
        pltpu.VMEM((2, 8, 16, 128), BF16),
        pltpu.VMEM((512, 1024), BF16),
        pltpu.VMEM((512, 1024), BF16),
        pltpu.VMEM((8, 32, 1024), BF16),
        pltpu.VMEM((512, 256), F32),
        pltpu.VMEM((512, 128), F32),
        pltpu.VMEM((384, 512), BF16),
        pltpu.VMEM((8, 384, 512), BF16),
        pltpu.VMEM((2, 4, 3, 128, 512), BF16),
        pltpu.VMEM((32, 1024), BF16),
        pltpu.VMEM((512, 128), F32),
        pltpu.VMEM((512, 128), F32),
        pltpu.VMEM((128, 512), F32),
        pltpu.SemaphoreType.DMA((N_SEND,)),
        pltpu.SemaphoreType.DMA((N_RECV,)),
        pltpu.SemaphoreType.DMA((12,)),
    ]
    shapes = (
        jax.ShapeDtypeStruct((32, 1024), BF16),
        jax.ShapeDtypeStruct((512, 128), F32),
        jax.ShapeDtypeStruct((512, 128), F32),
        jax.ShapeDtypeStruct((128, 512), F32),
    )
    results = pl.pallas_call(
        kernel,
        out_shape=shapes,
        in_specs=[any_spec, vmem, vmem] + [any_spec] * 7,
        out_specs=(any_spec,) * 4,
        scratch_shapes=scratch,
        compiler_params=pltpu.CompilerParams(
            collective_id=1, has_side_effects=True, vmem_limit_bytes=62 * 1024 * 1024
        ),
        cost_estimate=pl.CostEstimate(flops=5_000_000_000, bytes_accessed=12_000_000, transcendentals=400_000),
        name="distill_window",
    )(args[0], args[1].T, args[2].T, *args[3:])
    return pl.pallas_call(
        hand_over,
        out_shape=shapes,
        in_specs=[vmem] * 4,
        out_specs=(vmem,) * 4,
        compiler_params=pltpu.CompilerParams(vmem_limit_bytes=62 * 1024 * 1024),
        cost_estimate=pl.CostEstimate(flops=0, bytes_accessed=1_700_000, transcendentals=0),
        name="hand_over",
    )(*results)


def solution(mesh):
    in_specs = (
        P(("seq", "exp"), "tp"),
        P(("seq", "exp"), None),
        P(("seq", "exp"), None),
        P("exp", None, "tp"),
        P("exp", None, "tp"),
        P("exp", None, "tp"),
        P("seq", ("exp", "tp")),
        P("seq", ("exp", "tp")),
        P(("exp", "tp"), "seq"),
        P(("seq", "exp"), "tp"),
    )
    out_specs = (
        P(("seq", "exp"), "tp"),
        P("seq", ("exp", "tp")),
        P("seq", ("exp", "tp")),
        P(("exp", "tp"), "seq"),
    )
    return jax.shard_map(body, mesh=mesh, in_specs=in_specs, out_specs=out_specs, check_vma=False)
```

```python
import jax
import jax.numpy as jnp
from jax import lax
from jax.experimental import pallas as pl
from jax.experimental.pallas import tpu as pltpu
from jax.sharding import PartitionSpec as P

MESH = pl.DeviceIdType.MESH
F32 = jnp.float32
BF16 = jnp.bfloat16
Z_ORDER = (0, 1, 7, 2, 6, 3, 5, 4)
Z_POS = {z: i for i, z in enumerate(Z_ORDER)}
N_RECV = 400
N_SEND = 96


WAVES = ((0, 160), (320, 96))
Z_FIRST = 640


def row_at(pos, other=0):
    return other * 160 + pos * 32 if pos < 5 else 320 + other * 96 + (pos - 5) * 32


def row_of(z, other=0):
    return row_at(Z_POS[z % 8], other)


def sigmoid(a):
    return 1.0 / (1.0 + jnp.exp(-a))


class Agenda:
    def __init__(self):
        self.steps = []

    def at(self, time, step):
        self.steps.append((time, len(self.steps), step))

    def run(self):
        for _, _, step in sorted(self.steps, key=lambda s: (s[0], s[1])):
            step()


def kernel(
    tokens, ids, weights, egate, eup, edown, sgate, sup, sdown, ograd,
    t_hbm, gg_hbm, gu_hbm, gd_hbm,
    tok, act, dout, wt, wed, wgu, wd, hid, coef, part, sibp, rsb, gu, hg, gt, grad, ring, t_out, gg_out, gu_out, gd_out,
    send_sems, recv_sems, local_sems,
):
    yo = lax.axis_index("seq")
    eo = lax.axis_index("exp")
    xo = lax.axis_index("tp")
    zo = eo // 2
    co = lax.rem(eo, 2)

    def z_dev(d):
        return (yo, lax.rem(zo + d + 8, 8) * 2 + co, xo)

    def x_dev(d):
        return (yo, eo, lax.rem(xo + d + 4, 4))

    def y_dev(d):
        return (lax.rem(yo + d + 8, 8), eo, xo)

    sib = (yo, zo * 2 + (1 - co), xo)
    agenda = Agenda()
    drains = []
    counts = {"send": 0, "recv": 0, "local": 0}

    def new_send():
        counts["send"] += 1
        assert counts["send"] <= N_SEND
        return send_sems.at[counts["send"] - 1]

    def new_recv():
        counts["recv"] += 1
        assert counts["recv"] <= N_RECV
        return recv_sems.at[counts["recv"] - 1]

    def send(src, dst, s_sem, r_sem, device):
        pltpu.make_async_remote_copy(
            src_ref=src, dst_ref=dst, send_sem=s_sem, recv_sem=r_sem,
            device_id=device, device_id_type=MESH,
        ).start()

    def wait_recv(ref, r_sem):
        pltpu.make_async_remote_copy(
            src_ref=ref, dst_ref=ref, send_sem=send_sems.at[0], recv_sem=r_sem,
            device_id=sib, device_id_type=MESH,
        ).wait_recv()

    def drain(ref, s_sem):
        def step():
            pltpu.make_async_remote_copy(
                src_ref=ref, dst_ref=ref, send_sem=s_sem, recv_sem=recv_sems.at[0],
                device_id=sib, device_id_type=MESH,
            ).wait_send()

        drains.append(step)

    local = []

    def load(src, dst):
        copy = pltpu.make_async_copy(src, dst, local_sems.at[len(local)])
        copy.start()
        local.append(copy)
        return copy

    first = [
        load(tokens, tok.at[0, pl.ds(0, 32)]),
        load(sgate, wgu.at[pl.ds(pl.multiple_of(yo * 512, 512), 512), pl.ds(0, 128)]),
        load(sup, wgu.at[pl.ds(pl.multiple_of(yo * 512, 512), 512), pl.ds(128, 128)]),
        load(sdown, wd.at[yo]),
        load(ograd, dout.at[0, pl.ds(0, 32)]),
    ]
    stores = []

    def store(i, src, dst):
        copy = pltpu.make_async_copy(src, dst, local_sems.at[8 + i])
        copy.start()
        stores.append(copy)

    later = [
        load(egate.at[0], wt.at[:, pl.ds(0, 128)]),
        load(eup.at[0], wt.at[:, pl.ds(128, 128)]),
        load(edown.at[0], wed),
    ]

    barrier = pltpu.get_barrier_semaphore()
    peers = [z_dev(d) for d in range(1, 8)] + [x_dev(d) for d in range(1, 4)] + [y_dev(1), y_dev(-1), sib]
    for device in peers:
        pl.semaphore_signal(barrier, inc=1, device_id=device, device_id_type=MESH)

    lane = lax.broadcasted_iota(jnp.int32, (16, 128), 1)
    lane_e = lax.rem(lane, 16)
    lane_half = lax.rem(lane // 16, 2)
    blank = jnp.zeros((8, 96), jnp.int32)
    names = jnp.concatenate([ids[...], blank], axis=1).T
    shares = jnp.concatenate([weights[...], blank.astype(F32)], axis=1).T
    halves = []
    for half in range(2):
        total = jnp.zeros((16, 128), F32)
        for k in range(8):
            name = names[half * 16 : half * 16 + 16, k : k + 1]
            weight = shares[half * 16 : half * 16 + 16, k : k + 1]
            total = total + jnp.where(lane_e == name, weight, 0.0)
        halves.append(total)
    value = jnp.where(lane_half == 0, halves[0], halves[1])
    high = value.astype(BF16).astype(F32)
    value = jnp.where(lane < 32, high, jnp.where(lane < 64, value - high, 0.0))
    coef[0, 0] = value.astype(BF16)

    pl.semaphore_wait(barrier, len(peers))
    for copy in first:
        copy.wait()

    def gather(buf, t0, times=None):
        s_z0, s_x0, s_f0, s_b0 = new_send(), [new_send() for _ in range(2)], new_send(), new_send()
        s_x2, s_x1, s_z1, s_b1 = new_send(), new_send(), new_send(), new_send()
        pieces = ((0, 1), (1, 2), (3, 2), (5, 2), (7, 1))
        r_z0 = {(d, k): new_recv() for d in "RL" for k in range(1, 5)}
        r_x0 = {(rel, k): new_recv() for rel in (1, 3) for k in range(5)}
        r_f0 = {(rel, k): new_recv() for rel in (1, 3) for k in range(4)}
        r_x2 = new_recv()
        r_x1 = {rel: new_recv() for rel in (1, 2, 3)}
        r_z1 = {(d, k, c): new_recv() for d in "RL" for k in range(1, 5) for c in range(4)}
        r_b0, r_b1 = [new_recv() for _ in range(2)], [new_recv() for _ in range(2)]
        step_dev = {"R": z_dev(1), "L": z_dev(-1)}
        cols0, cols1 = pl.ds(0, Z_FIRST), pl.ds(Z_FIRST, 1024 - Z_FIRST)
        part_cols = {"R": pl.ds(0, 384), "L": pl.ds(384, Z_FIRST - 384)}

        def came(d, k):
            return (8 - k) % 8 if d == "R" else k % 8

        def z0_ref(z, d, k):
            return buf.at[0, pl.ds(row_of(z), 32), part_cols[d] if k == 4 else cols0]

        def z0_send(d, k, reach):
            device = z_dev(reach if d == "R" else -reach)
            send(z0_ref(came(d, k - reach), d, k), z0_ref(came(d, k), d, k), s_z0, r_z0[d, k], device)

        def piece_ref(rel, k, cols=cols0, other=0):
            pos, n = pieces[k]
            return buf.at[rel, pl.ds(row_at(pos, other), 32 * n), cols]

        def x0_piece(k):
            for i, d in enumerate((1, -1)):
                send(piece_ref(0, k), piece_ref((-d) % 4, k), s_x0[i], r_x0[(-d) % 4, k], x_dev(d))
            if k == 4:
                send(piece_ref(0, k), piece_ref(2, k), s_x2, r_x2, x_dev(2))

        def z1_ref(z, c):
            return buf.at[c, pl.ds(row_of(z), 32), cols1]

        def z1_send(d, k, c):
            send(z1_ref(came(d, k - 1), c), z1_ref(came(d, k), c), s_z1, r_z1[d, k, c], step_dev[d])

        def b0_send(rel, k):
            send(piece_ref(rel, k), piece_ref(rel, k, other=1), s_b0, r_b0[0 if k < 3 else 1], sib)

        def b1_send(z):
            send(
                buf.at[:, pl.ds(row_of(z), 32), cols1],
                buf.at[:, pl.ds(row_of(z, 1), 32), cols1],
                s_b1, r_b1[0 if Z_POS[z] < 5 else 1], sib,
            )

        plan = {("begin",): 0.0, ("x1",): 2.95, ("ready", 0): 12.24, ("ready", 1): 16.6}
        for k, (here, start, there, beyond) in enumerate(
            ((0, 0.01, 3.3, 11.6), (2.9, 2.91, 6.5, 11.6), (4.2, 4.21, 8.35, 12.0), (8.4, 8.41, 11.4, 15.3), (9.45, 9.46, 12.15, 15.35))
        ):
            plan["x0", k], plan["x0_done", k], plan["f0_done", k] = start, there, beyond
            if k:
                plan["z0", k] = here
                for c, when in ((0, 0.2 if k < 2 else 0.65), (1, 2.5), (3, 3.0), (2, 3.5)):
                    plan["z1", k, c] = 2.9 * k + when
        plan.update(times or {})

        def at(name, step):
            agenda.at(t0 + plan[name], step)

        def begin():
            for d in (1, -1, 2):
                send(z1_ref(0, 0), z1_ref(0, (-d) % 4), s_x1, r_x1[(-d) % 4], x_dev(d))
            for d in "RL":
                z0_send(d, 1, 1)
                z0_send(d, 2, 2)
            for d in "RL":
                z1_send(d, 1, 0)

        at(("begin",), begin)

        def z0_hop(k):
            for d in "RL":
                wait_recv(z0_ref(came(d, k), d, k), r_z0[d, k])
                if k == 2:
                    z0_send(d, 3, 1)
                    z0_send(d, 4, 2)

        def x0_start(k):
            x0_piece(k)
            b0_send(0, k)

        for k in range(1, 5):
            at(("z0", k), lambda k=k: z0_hop(k))
        for k in range(5):
            at(("x0", k), lambda k=k: x0_start(k))

        def x0_done(rel, k):
            wait_recv(piece_ref(rel, k), r_x0[rel, k])
            if k < 4:
                d, way = (1, "R") if rel == 3 else (-1, "L")
                send(
                    piece_ref(rel, k, part_cols[way]), piece_ref(2, k, part_cols[way]),
                    s_f0, r_f0[rel, k], x_dev(d),
                )
            b0_send(rel, k)

        def f0_done(k):
            if k == 4:
                wait_recv(piece_ref(2, k), r_x2)
            else:
                for rel, way in ((3, "R"), (1, "L")):
                    wait_recv(piece_ref(2, k, part_cols[way]), r_f0[rel, k])
            b0_send(2, k)

        for k in range(5):
            for rel in (1, 3):
                at(("x0_done", k), lambda rel=rel, k=k: x0_done(rel, k))
            at(("f0_done", k), lambda k=k: f0_done(k))

        def x1_done(rel):
            wait_recv(z1_ref(0, rel), r_x1[rel])
            for d in "RL":
                z1_send(d, 1, rel)
            if rel == 2:
                b1_send(0)

        for rel in (1, 3, 2):
            at(("x1",), lambda rel=rel: x1_done(rel))

        def z1_hop(k, c):
            for d in "RL":
                if k == 4 and (d == "R") != (c in (0, 1)):
                    continue
                z = came(d, k)
                wait_recv(z1_ref(z, c), r_z1[d, k, c])
                if k < 3 or (k == 3 and (d == "R") == (c in (0, 1))):
                    z1_send(d, k + 1, c)
                if c == 2:
                    b1_send(z)

        for k in range(1, 5):
            for c in (0, 1, 3, 2):
                at(("z1", k, c), lambda k=k, c=c: z1_hop(k, c))

        def finish(wave):
            first, n = WAVES[wave]
            rows = pl.ds(first + n, n)
            wait_recv(buf.at[:, rows, cols0], r_b0[wave])
            wait_recv(buf.at[:, rows, cols1], r_b1[wave])

        for wave in range(2):
            at(("ready", wave), lambda wave=wave: finish(wave))
        drain(buf.at[0, pl.ds(0, 224), cols0], s_z0)
        for sem in s_x0:
            drain(buf.at[0, pl.ds(0, 256), cols0], sem)
        drain(buf.at[0, pl.ds(0, 224), cols0], s_f0)
        drain(buf.at[0, pl.ds(0, 32), cols0], s_x2)
        drain(buf.at[:, pl.ds(0, 256), cols0], s_b0)
        drain(buf.at[pl.ds(1, 3), pl.ds(0, 32), cols1], s_x1)
        drain(buf.at[:, pl.ds(0, 224), cols1], s_z1)
        drain(buf.at[:, pl.ds(0, 256), cols1], s_b1)
        return [t0 + plan["ready", 0], t0 + plan["ready", 1]]

    s_yw = [new_send() for _ in range(3)]
    r_yw = {(d, k, a): new_recv() for d in "RL" for k in range(1, 5) for a in range(3)}

    def yw_ref(a, origin, d, k):
        if a < 2:
            start, n = origin * 512, 512
            if k == 4:
                start, n = start + (0 if d == "R" else 256), 256
            return wgu.at[pl.ds(pl.multiple_of(start, 256), n), pl.ds(a * 128, 128)]
        if k == 4:
            return wd.at[origin, pl.ds(0 if d == "R" else 64, 64)]
        return wd.at[origin]

    def yw_origin(d, k):
        return lax.rem(yo + (8 - k if d == "R" else k), 8)

    def yw_send(d, k, a):
        ref = yw_ref(a, yw_origin(d, k - 1), d, k)
        send(ref, ref, s_yw[a], r_yw[d, k, a], y_dev(1 if d == "R" else -1))

    def yw_start():
        for a in range(3):
            for d in "RL":
                yw_send(d, 1, a)

    def yw_hop(k, a):
        for d in "RL":
            wait_recv(yw_ref(a, yw_origin(d, k), d, k), r_yw[d, k, a])
            if k < 4:
                yw_send(d, k + 1, a)

    agenda.at(0.01, yw_start)
    yw_times = ((5.6, 6.1, 8.6), (11.4, 12.35, 13.46), (16.62, 20.35, 22.35), (23.05, 25.41, 26.05))
    for k in range(1, 5):
        for a in range(3):
            agenda.at(yw_times[k - 1][a], lambda k=k, a=a: yw_hop(k, a))
    drain(wgu.at[pl.ds(0, 3584), pl.ds(0, 128)], s_yw[0])
    drain(wgu.at[pl.ds(0, 3584), pl.ds(128, 128)], s_yw[1])
    drain(wd.at[pl.ds(0, 7)], s_yw[2])

    s_co, s_cb = new_send(), new_send()
    r_co = {z: new_recv() for z in range(1, 8)}
    r_cb = new_recv()

    def coef_start():
        for z in range(1, 8):
            send(coef.at[0, 0], coef.at[0, Z_POS[8 - z]], s_co, r_co[8 - z], z_dev(z))

    def coef_mirror():
        for z in range(1, 8):
            wait_recv(coef.at[0, Z_POS[z]], r_co[z])
        send(coef.at[0], coef.at[1], s_cb, r_cb, sib)

    agenda.at(4.0, coef_start)
    agenda.at(16.0, coef_mirror)
    drain(coef.at[0, pl.ds(0, 7)], s_co)
    drain(coef.at[0], s_cb)

    t_tok = gather(tok, 0.0)
    late = {("begin",): 12.22, ("x1",): 16.65, ("ready", 0): 35.2, ("ready", 1): 35.21}
    for k, (when, start, there, beyond) in enumerate(
        ((0, 16.68, 22.98, 35.13), (16.66, 20.3, 25.45, 35.13), (16.67, 22.96, 26.6, 35.13), (22.36, 22.97, 26.7, 35.13), (22.37, 22.98, 26.8, 35.13))
    ):
        late["x0", k], late["x0_done", k], late["f0_done", k] = start, there, beyond
        if k:
            late["z0", k] = when
            for c in range(4):
                late["z1", k, c] = (20.5, 25.4, 26.5, 35.12)[k - 1]
    gather(dout, 0.0, late)

    def weight_wait():
        for copy in later:
            copy.wait()

    agenda.at(t_tok[0] + 0.01, weight_wait)
    s_hid = [new_send() for _ in range(2)]
    r_hid = {(d, w): new_recv() for d in (1, 2, 3) for w in range(2)}

    def hid_cols(d):
        return pl.ds(pl.multiple_of(lax.rem(xo + d, 4) * 128, 128), 128)

    def project(buf, w, rows, out):
        out[rows, :] = jnp.dot(
            buf[0, rows, :],
            w[pl.ds(pl.multiple_of(xo * 1024, 1024), 1024), :],
            preferred_element_type=F32,
        )

        @pl.loop(1, 4)
        def _(rel):
            chunk = lax.rem(xo + rel, 4)
            out[rows, :] += jnp.dot(
                buf[rel, rows, :],
                w[pl.ds(pl.multiple_of(chunk * 1024, 1024), 1024), :],
                preferred_element_type=F32,
            )

    def wave_rows(wave):
        first, n = WAVES[wave]
        return pl.ds(first, 2 * n)

    def teacher_hidden(wave):
        rows = wave_rows(wave)
        project(tok, wt, rows, gu)
        gate = gu[rows, 0:128]
        up = gu[rows, 128:256]
        hid[rows, hid_cols(0)] = (gate * sigmoid(gate) * up).astype(BF16)
        ref = hid.at[rows, hid_cols(0)]
        for d in (1, 3, 2):
            send(ref, ref, s_hid[wave], r_hid[4 - d, wave], x_dev(d))

    for wave in range(2):
        agenda.at(t_tok[wave] + 0.02, lambda wave=wave: teacher_hidden(wave))
        drain(hid.at[wave_rows(wave), pl.ds(0, 384)], s_hid[wave])

    s_sp = [new_send() for _ in range(2)]
    r_sp = [new_recv() for _ in range(2)]
    s_rs = new_send()
    r_rs = {z: new_recv() for z in (1, 7)}
    r_rs.update({(z, turn): new_recv() for z in (2, 3, 5, 6) for turn in range(2)})
    r_rs4 = [new_recv() for _ in range(2)]

    def coef_column(other, wave):
        start, n = ((0, 5), (5, 3))[wave]
        lanes = lax.broadcasted_iota(jnp.int32, (n, 16, 128), 2)
        rows = coef[other, start : start + n].astype(F32)
        cols = []
        for half in range(2):
            wanted = (lanes == half * 16 + eo) | (lanes == 32 + half * 16 + eo)
            cols.append(jnp.sum(jnp.where(wanted, rows, 0.0), axis=2, keepdims=True))
        return jnp.concatenate(cols, axis=1).reshape(n * 32, 1)

    def hid_wait(wave):
        for d in (1, 3, 2):
            wait_recv(hid.at[wave_rows(wave), hid_cols(d)], r_hid[d, wave])
        if wave == 0:
            wait_recv(coef.at[1], r_cb)

    def teacher_down(wave, other):
        first, n = WAVES[wave]
        rows = pl.ds(first + other * n, n)
        own = pl.ds(first, n)
        scale = coef_column(other, wave)
        if other == 0:
            wait_recv(sibp.at[own], r_sp[wave])
        for q in range(2):
            cols = slice(q * 512, q * 512 + 512)
            res = jnp.dot(hid[rows, :], wed[:, cols], preferred_element_type=F32) * scale
            if other == 0:
                res = res + sibp[own, cols].astype(F32)
            part[rows, cols] = res.astype(BF16)
        if other == 1:
            send(part.at[rows], sibp.at[own], s_sp[wave], r_sp[wave], sib)
        else:
            if wave == 0:
                for z in (1, 7):
                    send(part.at[pl.ds(row_of(z), 32)], rsb.at[8 - z], s_rs, r_rs[8 - z], z_dev(z))
            else:
                for turn in range(2):
                    for z, step, i in ((3, 1, 0), (5, -1, 1)):
                        half = pl.ds(512 * (i ^ 1 ^ turn), 512)
                        send(
                            part.at[pl.ds(row_of(z), 32), half], rsb.at[8 - z, :, half],
                            s_rs, r_rs[8 - z, turn], z_dev(step),
                        )
                        if turn == 0:
                            half = pl.ds(512 * i, 512)
                            send(
                                part.at[pl.ds(row_of(4), 32), half], rsb.at[4, :, half],
                                s_rs, r_rs4[i], z_dev(2 * step),
                            )

    t_down = [20.2, 22.9]
    for wave in range(2):
        agenda.at(t_down[wave], lambda wave=wave: hid_wait(wave))
        for other in (1, 0):
            agenda.at(
                t_down[wave] + (0.1, 2.1)[1 - other],
                lambda wave=wave, other=other: teacher_down(wave, other),
            )
        first, n = WAVES[wave]
        drain(part.at[pl.ds(first + n, n)], s_sp[wave])
    drain(part.at[pl.ds(0, 224)], s_rs)

    def teacher_relay(turn):
        for i, (z, far) in enumerate(((2, 5), (6, 3))):
            start = 512 * (i ^ 1 ^ turn)
            half = pl.ds(start, 512)
            rows = pl.ds(row_of(z), 32)
            wait_recv(rsb.at[far, :, half], r_rs[far, turn])
            total = part[rows, half].astype(F32) + rsb[far, :, half].astype(F32)
            if turn == 1:
                wait_recv(rsb.at[4, :, half], r_rs4[i])
                total = total + rsb[4, :, half].astype(F32)
            part[rows, half] = total.astype(BF16)
            send(part.at[rows, half], rsb.at[8 - z, :, half], s_rs, r_rs[8 - z, turn], z_dev(z))

    for turn in range(2):
        agenda.at(26.0 + 0.1 * turn, lambda turn=turn: teacher_relay(turn))

    def teacher_sum():
        total = part[0:32, :].astype(F32)
        for z in (1, 7, 2, 6):
            if z in (1, 7):
                wait_recv(rsb.at[z], r_rs[z])
            else:
                for turn in range(2):
                    half = pl.ds(512 * ((0 if z == 6 else 1) ^ 1 ^ turn), 512)
                    wait_recv(rsb.at[z, :, half], r_rs[z, turn])
            total = total + rsb[z].astype(F32)
        row = total.astype(BF16)
        t_out[...] = row
        store(0, t_out, t_hbm)
        act[0, 0:32, :] = row

    t_sum = 35.0
    agenda.at(t_sum, teacher_sum)

    def student_back(rel):
        chunk = lax.rem(xo + rel, 4)
        total = jnp.zeros((512, 128), F32) if rel == 0 else hg[...]
        for j in range(2):
            total = total + lax.dot_general(
                dout[rel, :, j * 512 : j * 512 + 512],
                wd[chunk * 2 + j],
                (((1,), (1,)), ((), ())),
                preferred_element_type=F32,
            )
        hg[...] = total

    t_act = gather(act, t_sum + 0.1)
    for rel, when in enumerate((0.2, 0.2, 4.3, 4.3)):
        agenda.at(t_sum + 0.1 + when, lambda rel=rel: student_back(rel))

    def student_rows(wave):
        first, n = WAVES[wave]
        rows = pl.ds(first, 2 * n)
        project(act, wgu, rows, gu)
        gate = gu[rows, 0:128]
        up = gu[rows, 128:256]
        back = hg[rows, :]
        sig = sigmoid(gate)
        silu = gate * sig
        terms = (back * up * (sig * (1.0 + gate * (1.0 - sig))), back * silu, silu * up)
        for i, term in enumerate(terms):
            gt[i * 128 : i * 128 + 128, rows] = term.T.astype(BF16)

    for wave in range(2):
        agenda.at(t_act[wave] + 0.1, lambda wave=wave: student_rows(wave))

    s_yg = [new_send() for _ in range(3)]
    r_yg = {(d, k, a): new_recv() for d in "RL" for k in range(4) for a in range(3)}

    def term(k, a):
        owner = lax.rem(yo + k, 8)
        rel = lax.rem(owner // 2 - xo + 4, 4)
        cols = pl.ds(pl.multiple_of(lax.rem(owner, 2) * 512, 512), 512)
        if a == 0:
            grad[k, 0:256, :] = jnp.dot(
                gt[0:256, :], act[rel, :, cols], preferred_element_type=F32
            ).astype(BF16)
        else:
            grad[k, 256:384, :] = jnp.dot(
                gt[256:384, :], dout[rel, :, cols], preferred_element_type=F32
            ).astype(BF16)

    def yg_ref(d, k, a):
        if k == 0:
            return ring.at[0 if d == "R" else 1, 0, a, pl.ds(0 if d == "R" else 64, 64)]
        return ring.at[0 if d == "R" else 1, k, a]

    def yg_send(d, k, a):
        if k == 0:
            src = grad.at[4, pl.ds(a * 128 + (0 if d == "R" else 64), 64)]
        else:
            src = grad.at[4 - k if d == "R" else 4 + k, pl.ds(a * 128, 128)]
        send(src, yg_ref(d, k, a), s_yg[a], r_yg[d, k, a], y_dev(1 if d == "R" else -1))

    t_g = t_act[1] + 1.0

    def first_terms():
        term(4, 0)
        for a in range(2):
            for d in "RL":
                yg_send(d, 0, a)
        term(4, 1)
        for d in "RL":
            yg_send(d, 0, 2)
        for k in (3, 5):
            for a in range(2):
                term(k, a)

    agenda.at(t_g, first_terms)
    for i, k in enumerate((2, 6, 1, 7, 0)):
        for a in range(2):
            agenda.at(t_g + 8.0 + 3.2 * i + 1.5 * a, lambda k=k, a=a: term(k, a))

    def yg_hop(k, a):
        for d in "RL":
            wait_recv(yg_ref(d, k - 1, a), r_yg[d, k - 1, a])
            way = 0 if d == "R" else 1
            mine = 4 - k if d == "R" else 4 + k
            lo, n = a * 128, 128
            off = 0
            if k == 1:
                off, n = (0, 64) if d == "R" else (64, 64)
            grad[mine, lo + off : lo + off + n, :] = (
                grad[mine, lo + off : lo + off + n, :].astype(F32)
                + ring[way, k - 1, a, off : off + n, :].astype(F32)
            ).astype(BF16)
            yg_send(d, k, a)

    for k in range(1, 4):
        for a in range(3):
            agenda.at(t_g + 3.0 + 8.9 * (k - 1) + 2.95 * a, lambda k=k, a=a: yg_hop(k, a))

    def yg_last(a):
        for d in "RL":
            wait_recv(yg_ref(d, 3, a), r_yg[d, 3, a])
        total = (
            grad[0, a * 128 : a * 128 + 128, :].astype(F32)
            + ring[0, 3, a].astype(F32)
            + ring[1, 3, a].astype(F32)
        )
        if a == 0:
            gg_out[...] = total.T
            store(1, gg_out, gg_hbm)
        elif a == 1:
            gu_out[...] = total.T
            store(2, gu_out, gu_hbm)
        else:
            gd_out[...] = total
            store(3, gd_out, gd_hbm)

    for a in range(3):
        agenda.at(t_g + 3.0 + 8.9 * 3 + 2.95 * a, lambda a=a: yg_last(a))
        drain(grad.at[pl.ds(1, 7), pl.ds(a * 128, 128)], s_yg[a])

    agenda.run()
    for step in drains:
        step()
    for copy in stores:
        copy.wait()


def hand_over(*refs):
    for src, dst in zip(refs[:4], refs[4:]):
        dst[...] = src[...]


def body(*args):
    any_spec = pl.BlockSpec(memory_space=pl.ANY)
    vmem = pl.BlockSpec(memory_space=pltpu.VMEM)
    scratch = [
        pltpu.VMEM((4, 512, 1024), BF16),
        pltpu.VMEM((4, 512, 1024), BF16),
        pltpu.VMEM((4, 512, 1024), BF16),
        pltpu.VMEM((4096, 256), BF16),
        pltpu.VMEM((512, 1024), BF16),
        pltpu.VMEM((4096, 256), BF16),
        pltpu.VMEM((8, 128, 512), BF16),
        pltpu.VMEM((512, 512), BF16),
        pltpu.VMEM((2, 8, 16, 128), BF16),
        pltpu.VMEM((512, 1024), BF16),
        pltpu.VMEM((512, 1024), BF16),
        pltpu.VMEM((8, 32, 1024), BF16),
        pltpu.VMEM((512, 256), F32),
        pltpu.VMEM((512, 128), F32),
        pltpu.VMEM((384, 512), BF16),
        pltpu.VMEM((8, 384, 512), BF16),
        pltpu.VMEM((2, 4, 3, 128, 512), BF16),
        pltpu.VMEM((32, 1024), BF16),
        pltpu.VMEM((512, 128), F32),
        pltpu.VMEM((512, 128), F32),
        pltpu.VMEM((128, 512), F32),
        pltpu.SemaphoreType.DMA((N_SEND,)),
        pltpu.SemaphoreType.DMA((N_RECV,)),
        pltpu.SemaphoreType.DMA((12,)),
    ]
    shapes = (
        jax.ShapeDtypeStruct((32, 1024), BF16),
        jax.ShapeDtypeStruct((512, 128), F32),
        jax.ShapeDtypeStruct((512, 128), F32),
        jax.ShapeDtypeStruct((128, 512), F32),
    )
    results = pl.pallas_call(
        kernel,
        out_shape=shapes,
        in_specs=[any_spec, vmem, vmem] + [any_spec] * 7,
        out_specs=(any_spec,) * 4,
        scratch_shapes=scratch,
        compiler_params=pltpu.CompilerParams(
            collective_id=1, has_side_effects=True, vmem_limit_bytes=62 * 1024 * 1024
        ),
        cost_estimate=pl.CostEstimate(flops=5_000_000_000, bytes_accessed=12_000_000, transcendentals=400_000),
        name="distill_window",
    )(args[0], args[1].T, args[2].T, *args[3:])
    return pl.pallas_call(
        hand_over,
        out_shape=shapes,
        in_specs=[vmem] * 4,
        out_specs=(vmem,) * 4,
        compiler_params=pltpu.CompilerParams(vmem_limit_bytes=62 * 1024 * 1024),
        cost_estimate=pl.CostEstimate(flops=0, bytes_accessed=1_700_000, transcendentals=0),
        name="hand_over",
    )(*results)


def solution(mesh):
    in_specs = (
        P(("seq", "exp"), "tp"),
        P(("seq", "exp"), None),
        P(("seq", "exp"), None),
        P("exp", None, "tp"),
        P("exp", None, "tp"),
        P("exp", None, "tp"),
        P("seq", ("exp", "tp")),
        P("seq", ("exp", "tp")),
        P(("exp", "tp"), "seq"),
        P(("seq", "exp"), "tp"),
    )
    out_specs = (
        P(("seq", "exp"), "tp"),
        P("seq", ("exp", "tp")),
        P("seq", ("exp", "tp")),
        P(("exp", "tp"), "seq"),
    )
    return jax.shard_map(body, mesh=mesh, in_specs=in_specs, out_specs=out_specs, check_vma=False)
```

```python
import jax
import jax.numpy as jnp
from jax import lax
from jax.experimental import pallas as pl
from jax.experimental.pallas import tpu as pltpu
from jax.sharding import PartitionSpec as P

MESH = pl.DeviceIdType.MESH
F32 = jnp.float32
BF16 = jnp.bfloat16
Z_ORDER = (0, 1, 7, 2, 6, 3, 5, 4)
Z_POS = {z: i for i, z in enumerate(Z_ORDER)}
N_RECV = 280
N_SEND = 40


WAVES = ((0, 160), (320, 96))
Z_FIRST = 640


def row_at(pos, other=0):
    return other * 160 + pos * 32 if pos < 5 else 320 + other * 96 + (pos - 5) * 32


def row_of(z, other=0):
    return row_at(Z_POS[z % 8], other)


def sigmoid(a):
    return 1.0 / (1.0 + jnp.exp(-a))


class Agenda:
    def __init__(self):
        self.steps = []

    def at(self, time, step):
        self.steps.append((time, len(self.steps), step))

    def run(self):
        for _, _, step in sorted(self.steps, key=lambda s: (s[0], s[1])):
            step()


def kernel(
    tokens, ids, weights, egate, eup, edown, sgate, sup, sdown, ograd,
    t_hbm, gg_hbm, gu_hbm, gd_hbm,
    tok, act, dout, wt, wed, wgu, wd, hid, coef, part, sibp, rsb, gu, hg, gt, grad, ring, t_out, gg_out, gu_out, gd_out, ids_v, weights_v,
    send_sems, recv_sems, local_sems,
):
    yo = lax.axis_index("seq")
    eo = lax.axis_index("exp")
    xo = lax.axis_index("tp")
    zo = eo // 2
    co = lax.rem(eo, 2)

    def z_dev(d):
        return (yo, lax.rem(zo + d + 8, 8) * 2 + co, xo)

    def x_dev(d):
        return (yo, eo, lax.rem(xo + d + 4, 4))

    def y_dev(d):
        return (lax.rem(yo + d + 8, 8), eo, xo)

    sib = (yo, zo * 2 + (1 - co), xo)
    agenda = Agenda()
    drains = []
    counts = {"send": 0, "recv": 0, "local": 0}

    def new_send():
        counts["send"] += 1
        assert counts["send"] <= N_SEND
        return send_sems.at[counts["send"] - 1]

    def new_recv():
        counts["recv"] += 1
        assert counts["recv"] <= N_RECV
        return recv_sems.at[counts["recv"] - 1]

    def send(src, dst, s_sem, r_sem, device):
        pltpu.make_async_remote_copy(
            src_ref=src, dst_ref=dst, send_sem=s_sem, recv_sem=r_sem,
            device_id=device, device_id_type=MESH,
        ).start()

    def wait_recv(ref, r_sem):
        pltpu.make_async_remote_copy(
            src_ref=ref, dst_ref=ref, send_sem=send_sems.at[0], recv_sem=r_sem,
            device_id=sib, device_id_type=MESH,
        ).wait_recv()

    def drain(ref, s_sem):
        def step():
            pltpu.make_async_remote_copy(
                src_ref=ref, dst_ref=ref, send_sem=s_sem, recv_sem=recv_sems.at[0],
                device_id=sib, device_id_type=MESH,
            ).wait_send()

        drains.append(step)

    barrier = pltpu.get_barrier_semaphore()
    peers = [z_dev(d) for d in range(1, 8)] + [x_dev(d) for d in range(1, 4)] + [y_dev(1), y_dev(-1), sib]
    for device in peers:
        pl.semaphore_signal(barrier, inc=1, device_id=device, device_id_type=MESH)

    local = []

    def load(src, dst):
        copy = pltpu.make_async_copy(src, dst, local_sems.at[len(local)])
        copy.start()
        local.append(copy)
        return copy

    first = [
        load(tokens, tok.at[0, pl.ds(0, 32)]),
        load(sgate, wgu.at[pl.ds(pl.multiple_of(yo * 512, 512), 512), pl.ds(0, 128)]),
        load(sup, wgu.at[pl.ds(pl.multiple_of(yo * 512, 512), 512), pl.ds(128, 128)]),
        load(sdown, wd.at[yo]),
        load(ograd, dout.at[0, pl.ds(0, 32)]),
    ]
    routes = [load(ids, ids_v), load(weights, weights_v)]
    stores = []

    def store(i, src, dst):
        copy = pltpu.make_async_copy(src, dst, local_sems.at[10 + i])
        copy.start()
        stores.append(copy)

    later = [
        load(egate.at[0], wt.at[:, pl.ds(0, 128)]),
        load(eup.at[0], wt.at[:, pl.ds(128, 128)]),
        load(edown.at[0], wed),
    ]

    pl.semaphore_wait(barrier, len(peers))
    for copy in first:
        copy.wait()

    def gather(buf, t0, times=None):
        s_z0, s_x0, s_f0, s_b0 = new_send(), [new_send() for _ in range(2)], new_send(), new_send()
        s_x2, s_x1, s_z1, s_b1 = new_send(), new_send(), new_send(), new_send()
        pieces = ((0, 1), (1, 2), (3, 2), (5, 2), (7, 1))
        r_z0 = {(d, k): new_recv() for d in "RL" for k in range(1, 5)}
        r_x0 = {(rel, k): new_recv() for rel in (1, 3) for k in range(5)}
        r_f0 = {(rel, k): new_recv() for rel in (1, 3) for k in range(4)}
        r_x2 = new_recv()
        r_x1 = {rel: new_recv() for rel in (1, 2, 3)}
        r_z1 = {(d, k, c): new_recv() for d in "RL" for k in range(1, 5) for c in range(4)}
        r_b0, r_b1 = [new_recv() for _ in range(2)], [new_recv() for _ in range(2)]
        step_dev = {"R": z_dev(1), "L": z_dev(-1)}
        cols0, cols1 = pl.ds(0, Z_FIRST), pl.ds(Z_FIRST, 1024 - Z_FIRST)
        part_cols = {"R": pl.ds(0, 384), "L": pl.ds(384, Z_FIRST - 384)}

        def came(d, k):
            return (8 - k) % 8 if d == "R" else k % 8

        def z0_ref(z, d, k):
            return buf.at[0, pl.ds(row_of(z), 32), part_cols[d] if k == 4 else cols0]

        def z0_send(d, k, reach):
            device = z_dev(reach if d == "R" else -reach)
            send(z0_ref(came(d, k - reach), d, k), z0_ref(came(d, k), d, k), s_z0, r_z0[d, k], device)

        def piece_ref(rel, k, cols=cols0, other=0):
            pos, n = pieces[k]
            return buf.at[rel, pl.ds(row_at(pos, other), 32 * n), cols]

        def x0_piece(k):
            for i, d in enumerate((1, -1)):
                send(piece_ref(0, k), piece_ref((-d) % 4, k), s_x0[i], r_x0[(-d) % 4, k], x_dev(d))
            if k == 4:
                send(piece_ref(0, k), piece_ref(2, k), s_x2, r_x2, x_dev(2))

        def z1_ref(z, c):
            return buf.at[c, pl.ds(row_of(z), 32), cols1]

        def z1_send(d, k, c):
            send(z1_ref(came(d, k - 1), c), z1_ref(came(d, k), c), s_z1, r_z1[d, k, c], step_dev[d])

        def b0_send(rel, k):
            send(piece_ref(rel, k), piece_ref(rel, k, other=1), s_b0, r_b0[0 if k < 3 else 1], sib)

        def b1_send(z):
            send(
                buf.at[:, pl.ds(row_of(z), 32), cols1],
                buf.at[:, pl.ds(row_of(z, 1), 32), cols1],
                s_b1, r_b1[0 if Z_POS[z] < 5 else 1], sib,
            )

        plan = {("begin",): 0.0, ("x1",): 2.95, ("ready", 0): 12.24, ("ready", 1): 16.6}
        for k, (here, start, there, beyond) in enumerate(
            ((0, 0.01, 3.3, 11.6), (2.9, 2.91, 6.5, 11.6), (4.2, 4.21, 8.35, 12.0), (8.4, 8.41, 11.4, 15.3), (9.45, 9.46, 12.15, 15.35))
        ):
            plan["x0", k], plan["x0_done", k], plan["f0_done", k] = start, there, beyond
            if k:
                plan["z0", k] = here
                for c, when in ((0, 0.2 if k < 2 else 0.65), (1, 2.5), (3, 3.0), (2, 3.5)):
                    plan["z1", k, c] = 2.9 * k + when
        plan.update(times or {})

        def at(name, step):
            agenda.at(t0 + plan[name], step)

        def begin():
            for d in (1, -1, 2):
                send(z1_ref(0, 0), z1_ref(0, (-d) % 4), s_x1, r_x1[(-d) % 4], x_dev(d))
            for d in "RL":
                z0_send(d, 1, 1)
                z0_send(d, 2, 2)
            for d in "RL":
                z1_send(d, 1, 0)

        at(("begin",), begin)

        def z0_hop(k):
            for d in "RL":
                wait_recv(z0_ref(came(d, k), d, k), r_z0[d, k])
                if k == 2:
                    z0_send(d, 3, 1)
                    z0_send(d, 4, 2)

        def x0_start(k):
            x0_piece(k)
            b0_send(0, k)

        for k in range(1, 5):
            at(("z0", k), lambda k=k: z0_hop(k))
        for k in range(5):
            at(("x0", k), lambda k=k: x0_start(k))

        def x0_done(rel, k):
            wait_recv(piece_ref(rel, k), r_x0[rel, k])
            if k < 4:
                d, way = (1, "R") if rel == 3 else (-1, "L")
                send(
                    piece_ref(rel, k, part_cols[way]), piece_ref(2, k, part_cols[way]),
                    s_f0, r_f0[rel, k], x_dev(d),
                )
            b0_send(rel, k)

        def f0_done(k):
            if k == 4:
                wait_recv(piece_ref(2, k), r_x2)
            else:
                for rel, way in ((3, "R"), (1, "L")):
                    wait_recv(piece_ref(2, k, part_cols[way]), r_f0[rel, k])
            b0_send(2, k)

        for k in range(5):
            for rel in (1, 3):
                at(("x0_done", k), lambda rel=rel, k=k: x0_done(rel, k))
            at(("f0_done", k), lambda k=k: f0_done(k))

        def x1_done(rel):
            wait_recv(z1_ref(0, rel), r_x1[rel])
            for d in "RL":
                z1_send(d, 1, rel)
            if rel == 2:
                b1_send(0)

        for rel in (1, 3, 2):
            at(("x1",), lambda rel=rel: x1_done(rel))

        def z1_hop(k, c):
            for d in "RL":
                if k == 4 and (d == "R") != (c in (0, 1)):
                    continue
                z = came(d, k)
                wait_recv(z1_ref(z, c), r_z1[d, k, c])
                if k < 3 or (k == 3 and (d == "R") == (c in (0, 1))):
                    z1_send(d, k + 1, c)
                if c == 2:
                    b1_send(z)

        for k in range(1, 5):
            for c in (0, 1, 3, 2):
                at(("z1", k, c), lambda k=k, c=c: z1_hop(k, c))

        def finish(wave):
            first, n = WAVES[wave]
            rows = pl.ds(first + n, n)
            wait_recv(buf.at[:, rows, cols0], r_b0[wave])
            wait_recv(buf.at[:, rows, cols1], r_b1[wave])

        for wave in range(2):
            at(("ready", wave), lambda wave=wave: finish(wave))
        drain(buf.at[0, pl.ds(0, 224), cols0], s_z0)
        for sem in s_x0:
            drain(buf.at[0, pl.ds(0, 256), cols0], sem)
        drain(buf.at[0, pl.ds(0, 224), cols0], s_f0)
        drain(buf.at[0, pl.ds(0, 32), cols0], s_x2)
        drain(buf.at[:, pl.ds(0, 256), cols0], s_b0)
        drain(buf.at[pl.ds(1, 3), pl.ds(0, 32), cols1], s_x1)
        drain(buf.at[:, pl.ds(0, 224), cols1], s_z1)
        drain(buf.at[:, pl.ds(0, 256), cols1], s_b1)
        return [t0 + plan["ready", 0], t0 + plan["ready", 1]]

    s_yw = [new_send() for _ in range(3)]
    r_yw = {(d, k, a): new_recv() for d in "RL" for k in range(1, 5) for a in range(3)}

    def yw_ref(a, origin, d, k):
        if a < 2:
            start, n = origin * 512, 512
            if k == 4:
                start, n = start + (0 if d == "R" else 256), 256
            return wgu.at[pl.ds(pl.multiple_of(start, 256), n), pl.ds(a * 128, 128)]
        if k == 4:
            return wd.at[origin, pl.ds(0 if d == "R" else 64, 64)]
        return wd.at[origin]

    def yw_origin(d, k):
        return lax.rem(yo + (8 - k if d == "R" else k), 8)

    def yw_send(d, k, a):
        ref = yw_ref(a, yw_origin(d, k - 1), d, k)
        send(ref, ref, s_yw[a], r_yw[d, k, a], y_dev(1 if d == "R" else -1))

    def yw_start():
        for a in range(3):
            for d in "RL":
                yw_send(d, 1, a)

    def yw_hop(k, a):
        for d in "RL":
            wait_recv(yw_ref(a, yw_origin(d, k), d, k), r_yw[d, k, a])
            if k < 4:
                yw_send(d, k + 1, a)

    agenda.at(0.01, yw_start)
    yw_times = ((5.6, 6.1, 8.6), (11.4, 12.35, 13.46), (16.62, 20.35, 23.11), (25.46, 26.05, 26.65))
    for k in range(1, 5):
        for a in range(3):
            agenda.at(yw_times[k - 1][a], lambda k=k, a=a: yw_hop(k, a))
    drain(wgu.at[pl.ds(0, 3584), pl.ds(0, 128)], s_yw[0])
    drain(wgu.at[pl.ds(0, 3584), pl.ds(128, 128)], s_yw[1])
    drain(wd.at[pl.ds(0, 7)], s_yw[2])

    s_co, s_cb = new_send(), new_send()
    r_co = {z: new_recv() for z in range(1, 8)}
    r_cb = new_recv()

    def coef_start():
        for copy in routes:
            copy.wait()
        lane = lax.broadcasted_iota(jnp.int32, (16, 128), 1)
        lane_e = lax.rem(lane, 16)
        lane_half = lax.rem(lane // 16, 2)
        blank = jnp.zeros((8, 96), jnp.int32)
        names = jnp.concatenate([ids_v[...], blank], axis=1).T
        shares = jnp.concatenate([weights_v[...], blank.astype(F32)], axis=1).T
        halves = []
        for half in range(2):
            total = jnp.zeros((16, 128), F32)
            for k in range(8):
                name = names[half * 16 : half * 16 + 16, k : k + 1]
                weight = shares[half * 16 : half * 16 + 16, k : k + 1]
                total = total + jnp.where(lane_e == name, weight, 0.0)
            halves.append(total)
        value = jnp.where(lane_half == 0, halves[0], halves[1])
        high = value.astype(BF16).astype(F32)
        value = jnp.where(lane < 32, high, jnp.where(lane < 64, value - high, 0.0))
        coef[0, 0] = value.astype(BF16)
        for z in range(1, 8):
            send(coef.at[0, 0], coef.at[0, Z_POS[8 - z]], s_co, r_co[8 - z], z_dev(z))

    def coef_mirror():
        for z in range(1, 8):
            wait_recv(coef.at[0, Z_POS[z]], r_co[z])
        send(coef.at[0], coef.at[1], s_cb, r_cb, sib)

    agenda.at(4.0, coef_start)
    agenda.at(16.0, coef_mirror)
    drain(coef.at[0, pl.ds(0, 7)], s_co)
    drain(coef.at[0], s_cb)

    t_tok = gather(tok, 0.0)
    late = {("begin",): 12.22, ("x1",): 16.55, ("ready", 0): 35.2, ("ready", 1): 35.21}
    for k, (when, start, there, beyond) in enumerate(
        ((0, 16.69, 23.12, 35.13), (16.56, 20.3, 25.45, 35.13), (16.68, 22.96, 26.6, 35.13), (25.41, 25.42, 26.7, 35.13), (25.41, 25.43, 26.8, 35.13))
    ):
        late["x0", k], late["x0_done", k], late["f0_done", k] = start, there, beyond
        if k:
            late["z0", k] = when
            for c in range(4):
                late["z1", k, c] = (20.5, 23.1, 26.5, 35.12)[k - 1]
    gather(dout, 0.0, late)

    def weight_wait():
        for copy in later:
            copy.wait()

    agenda.at(t_tok[0] + 0.01, weight_wait)
    s_hid = [new_send() for _ in range(2)]
    r_hid = {(d, w, other): new_recv() for d in (1, 2, 3) for w in range(2) for other in range(2)}

    def hid_cols(d):
        return pl.ds(pl.multiple_of(lax.rem(xo + d, 4) * 128, 128), 128)

    def project(buf, w, rows, out):
        out[rows, :] = jnp.dot(
            buf[0, rows, :],
            w[pl.ds(pl.multiple_of(xo * 1024, 1024), 1024), :],
            preferred_element_type=F32,
        )

        @pl.loop(1, 4)
        def _(rel):
            chunk = lax.rem(xo + rel, 4)
            out[rows, :] += jnp.dot(
                buf[rel, rows, :],
                w[pl.ds(pl.multiple_of(chunk * 1024, 1024), 1024), :],
                preferred_element_type=F32,
            )

    def wave_rows(wave):
        first, n = WAVES[wave]
        return pl.ds(first, 2 * n)

    def teacher_hidden(wave):
        rows = wave_rows(wave)
        project(tok, wt, rows, gu)
        gate = gu[rows, 0:128]
        up = gu[rows, 128:256]
        hid[rows, hid_cols(0)] = (gate * sigmoid(gate) * up).astype(BF16)
        first, n = WAVES[wave]
        for other in (1, 0):
            ref = hid.at[pl.ds(first + other * n, n), hid_cols(0)]
            for d in (1, 3, 2):
                send(ref, ref, s_hid[wave], r_hid[4 - d, wave, other], x_dev(d))

    for wave in range(2):
        agenda.at(t_tok[wave] + 0.02, lambda wave=wave: teacher_hidden(wave))
        drain(hid.at[wave_rows(wave), pl.ds(0, 384)], s_hid[wave])

    s_sp = [new_send() for _ in range(2)]
    r_sp = [new_recv() for _ in range(2)]
    s_rs = new_send()
    r_rs = {z: new_recv() for z in (1, 7)}
    r_rs.update({(z, turn): new_recv() for z in (2, 3, 5, 6) for turn in range(2)})
    r_rs4 = [new_recv() for _ in range(2)]

    def coef_column(other, wave):
        start, n = ((0, 5), (5, 3))[wave]
        lanes = lax.broadcasted_iota(jnp.int32, (n, 16, 128), 2)
        rows = coef[other, start : start + n].astype(F32)
        cols = []
        for half in range(2):
            wanted = (lanes == half * 16 + eo) | (lanes == 32 + half * 16 + eo)
            cols.append(jnp.sum(jnp.where(wanted, rows, 0.0), axis=2, keepdims=True))
        return jnp.concatenate(cols, axis=1).reshape(n * 32, 1)

    def hid_wait(wave):
        if wave == 0:
            wait_recv(coef.at[1], r_cb)

    def teacher_down(wave, other):
        first, n = WAVES[wave]
        rows = pl.ds(first + other * n, n)
        own = pl.ds(first, n)
        scale = coef_column(other, wave)
        for d in (1, 3, 2):
            wait_recv(hid.at[rows, hid_cols(d)], r_hid[d, wave, other])
        if other == 0:
            wait_recv(sibp.at[own], r_sp[wave])
        for q in range(2):
            cols = slice(q * 512, q * 512 + 512)
            res = jnp.dot(hid[rows, :], wed[:, cols], preferred_element_type=F32) * scale
            if other == 0:
                res = res + sibp[own, cols].astype(F32)
            part[rows, cols] = res.astype(BF16)
        if other == 1:
            send(part.at[rows], sibp.at[own], s_sp[wave], r_sp[wave], sib)
        else:
            if wave == 0:
                for z in (1, 7):
                    send(part.at[pl.ds(row_of(z), 32)], rsb.at[8 - z], s_rs, r_rs[8 - z], z_dev(z))
            else:
                for turn in range(2):
                    for z, step, i in ((3, 1, 0), (5, -1, 1)):
                        half = pl.ds(512 * (i ^ 1 ^ turn), 512)
                        send(
                            part.at[pl.ds(row_of(z), 32), half], rsb.at[8 - z, :, half],
                            s_rs, r_rs[8 - z, turn], z_dev(step),
                        )
                        if turn == 0:
                            half = pl.ds(512 * i, 512)
                            send(
                                part.at[pl.ds(row_of(4), 32), half], rsb.at[4, :, half],
                                s_rs, r_rs4[i], z_dev(2 * step),
                            )

    t_down = [20.2, 22.9]
    for wave in range(2):
        agenda.at(t_down[wave], lambda wave=wave: hid_wait(wave))
        for other in (1, 0):
            agenda.at(
                t_down[wave] + (0.1, 2.1)[1 - other],
                lambda wave=wave, other=other: teacher_down(wave, other),
            )
        first, n = WAVES[wave]
        drain(part.at[pl.ds(first + n, n)], s_sp[wave])
    drain(part.at[pl.ds(0, 224)], s_rs)

    def teacher_relay(turn):
        for i, (z, far) in enumerate(((2, 5), (6, 3))):
            start = 512 * (i ^ 1 ^ turn)
            half = pl.ds(start, 512)
            rows = pl.ds(row_of(z), 32)
            wait_recv(rsb.at[far, :, half], r_rs[far, turn])
            total = part[rows, half].astype(F32) + rsb[far, :, half].astype(F32)
            if turn == 1:
                wait_recv(rsb.at[4, :, half], r_rs4[i])
                total = total + rsb[4, :, half].astype(F32)
            part[rows, half] = total.astype(BF16)
            send(part.at[rows, half], rsb.at[8 - z, :, half], s_rs, r_rs[8 - z, turn], z_dev(z))

    for turn in range(2):
        agenda.at(26.0 + 0.1 * turn, lambda turn=turn: teacher_relay(turn))

    def teacher_sum():
        total = part[0:32, :].astype(F32)
        for z in (1, 7, 2, 6):
            if z in (1, 7):
                wait_recv(rsb.at[z], r_rs[z])
            else:
                for turn in range(2):
                    half = pl.ds(512 * ((0 if z == 6 else 1) ^ 1 ^ turn), 512)
                    wait_recv(rsb.at[z, :, half], r_rs[z, turn])
            total = total + rsb[z].astype(F32)
        row = total.astype(BF16)
        t_out[...] = row
        store(0, t_out, t_hbm)
        act[0, 0:32, :] = row

    t_sum = 35.0
    agenda.at(t_sum, teacher_sum)

    def student_back(rel):
        chunk = lax.rem(xo + rel, 4)
        total = jnp.zeros((512, 128), F32) if rel == 0 else hg[...]
        for j in range(2):
            total = total + lax.dot_general(
                dout[rel, :, j * 512 : j * 512 + 512],
                wd[chunk * 2 + j],
                (((1,), (1,)), ((), ())),
                preferred_element_type=F32,
            )
        hg[...] = total

    t_act = gather(act, t_sum + 0.1)
    for rel, when in enumerate((0.2, 0.2, 6.55, 6.55)):
        agenda.at(t_sum + 0.1 + when, lambda rel=rel: student_back(rel))

    def student_rows(wave):
        first, n = WAVES[wave]
        rows = pl.ds(first, 2 * n)
        project(act, wgu, rows, gu)
        gate = gu[rows, 0:128]
        up = gu[rows, 128:256]
        back = hg[rows, :]
        sig = sigmoid(gate)
        silu = gate * sig
        terms = (back * up * (sig * (1.0 + gate * (1.0 - sig))), back * silu, silu * up)
        for i, term in enumerate(terms):
            gt[i * 128 : i * 128 + 128, rows] = term.T.astype(BF16)

    for wave in range(2):
        agenda.at(t_act[wave] + 0.1, lambda wave=wave: student_rows(wave))

    s_yg = [new_send() for _ in range(3)]
    r_yg = {(d, k, a): new_recv() for d in "RL" for k in range(4) for a in range(3)}

    def term(k, a):
        owner = lax.rem(yo + k, 8)
        rel = lax.rem(owner // 2 - xo + 4, 4)
        cols = pl.ds(pl.multiple_of(lax.rem(owner, 2) * 512, 512), 512)
        if a == 0:
            grad[k, 0:256, :] = jnp.dot(
                gt[0:256, :], act[rel, :, cols], preferred_element_type=F32
            ).astype(BF16)
        else:
            grad[k, 256:384, :] = jnp.dot(
                gt[256:384, :], dout[rel, :, cols], preferred_element_type=F32
            ).astype(BF16)

    def yg_ref(d, k, a):
        if k == 0:
            return ring.at[0 if d == "R" else 1, 0, a, pl.ds(0 if d == "R" else 64, 64)]
        return ring.at[0 if d == "R" else 1, k, a]

    def yg_send(d, k, a):
        if k == 0:
            src = grad.at[4, pl.ds(a * 128 + (0 if d == "R" else 64), 64)]
        else:
            src = grad.at[4 - k if d == "R" else 4 + k, pl.ds(a * 128, 128)]
        send(src, yg_ref(d, k, a), s_yg[a], r_yg[d, k, a], y_dev(1 if d == "R" else -1))

    t_g = t_act[1] + 1.0

    def first_terms():
        term(4, 0)
        for a in range(2):
            for d in "RL":
                yg_send(d, 0, a)
        term(4, 1)
        for d in "RL":
            yg_send(d, 0, 2)
        for k in (3, 5):
            for a in range(2):
                term(k, a)

    agenda.at(t_g, first_terms)
    for i, k in enumerate((2, 6, 1, 7, 0)):
        for a in range(2):
            agenda.at(t_g + 8.0 + 3.2 * i + 1.5 * a, lambda k=k, a=a: term(k, a))

    def yg_hop(k, a):
        for d in "RL":
            wait_recv(yg_ref(d, k - 1, a), r_yg[d, k - 1, a])
            way = 0 if d == "R" else 1
            mine = 4 - k if d == "R" else 4 + k
            lo, n = a * 128, 128
            off = 0
            if k == 1:
                off, n = (0, 64) if d == "R" else (64, 64)
            grad[mine, lo + off : lo + off + n, :] = (
                grad[mine, lo + off : lo + off + n, :].astype(F32)
                + ring[way, k - 1, a, off : off + n, :].astype(F32)
            ).astype(BF16)
            yg_send(d, k, a)

    for k in range(1, 4):
        for a in range(3):
            agenda.at(t_g + 3.0 + 8.9 * (k - 1) + 2.95 * a, lambda k=k, a=a: yg_hop(k, a))

    def yg_last(a):
        for d in "RL":
            wait_recv(yg_ref(d, 3, a), r_yg[d, 3, a])
        total = (
            grad[0, a * 128 : a * 128 + 128, :].astype(F32)
            + ring[0, 3, a].astype(F32)
            + ring[1, 3, a].astype(F32)
        )
        if a == 0:
            gg_out[...] = total.T
            store(1, gg_out, gg_hbm)
        elif a == 1:
            gu_out[...] = total.T
            store(2, gu_out, gu_hbm)
        else:
            gd_out[...] = total
            store(3, gd_out, gd_hbm)

    for a in range(3):
        agenda.at(t_g + 3.0 + 8.9 * 3 + 2.95 * a, lambda a=a: yg_last(a))
        drain(grad.at[pl.ds(1, 7), pl.ds(a * 128, 128)], s_yg[a])

    agenda.run()
    for step in drains:
        step()
    for copy in stores:
        copy.wait()


def hand_over(*refs):
    for src, dst in zip(refs[:4], refs[4:]):
        dst[...] = src[...]


def body(*args):
    any_spec = pl.BlockSpec(memory_space=pl.ANY)
    vmem = pl.BlockSpec(memory_space=pltpu.VMEM)
    scratch = [
        pltpu.VMEM((4, 512, 1024), BF16),
        pltpu.VMEM((4, 512, 1024), BF16),
        pltpu.VMEM((4, 512, 1024), BF16),
        pltpu.VMEM((4096, 256), BF16),
        pltpu.VMEM((512, 1024), BF16),
        pltpu.VMEM((4096, 256), BF16),
        pltpu.VMEM((8, 128, 512), BF16),
        pltpu.VMEM((512, 512), BF16),
        pltpu.VMEM((2, 8, 16, 128), BF16),
        pltpu.VMEM((512, 1024), BF16),
        pltpu.VMEM((512, 1024), BF16),
        pltpu.VMEM((8, 32, 1024), BF16),
        pltpu.VMEM((512, 256), F32),
        pltpu.VMEM((512, 128), F32),
        pltpu.VMEM((384, 512), BF16),
        pltpu.VMEM((8, 384, 512), BF16),
        pltpu.VMEM((2, 4, 3, 128, 512), BF16),
        pltpu.VMEM((32, 1024), BF16),
        pltpu.VMEM((512, 128), F32),
        pltpu.VMEM((512, 128), F32),
        pltpu.VMEM((128, 512), F32),
        pltpu.VMEM((8, 32), jnp.int32),
        pltpu.VMEM((8, 32), F32),
        pltpu.SemaphoreType.DMA((N_SEND,)),
        pltpu.SemaphoreType.DMA((N_RECV,)),
        pltpu.SemaphoreType.DMA((14,)),
    ]
    shapes = (
        jax.ShapeDtypeStruct((32, 1024), BF16),
        jax.ShapeDtypeStruct((512, 128), F32),
        jax.ShapeDtypeStruct((512, 128), F32),
        jax.ShapeDtypeStruct((128, 512), F32),
    )
    results = pl.pallas_call(
        kernel,
        out_shape=shapes,
        in_specs=[any_spec] * 10,
        out_specs=(any_spec,) * 4,
        scratch_shapes=scratch,
        compiler_params=pltpu.CompilerParams(
            collective_id=1, has_side_effects=True, vmem_limit_bytes=62 * 1024 * 1024
        ),
        cost_estimate=pl.CostEstimate(flops=5_000_000_000, bytes_accessed=12_000_000, transcendentals=400_000),
        name="distill_window",
    )(args[0], args[1].T, args[2].T, *args[3:])
    return pl.pallas_call(
        hand_over,
        out_shape=shapes,
        in_specs=[vmem] * 4,
        out_specs=(vmem,) * 4,
        compiler_params=pltpu.CompilerParams(vmem_limit_bytes=62 * 1024 * 1024),
        cost_estimate=pl.CostEstimate(flops=0, bytes_accessed=1_700_000, transcendentals=0),
        name="hand_over",
    )(*results)


def solution(mesh):
    in_specs = (
        P(("seq", "exp"), "tp"),
        P(("seq", "exp"), None),
        P(("seq", "exp"), None),
        P("exp", None, "tp"),
        P("exp", None, "tp"),
        P("exp", None, "tp"),
        P("seq", ("exp", "tp")),
        P("seq", ("exp", "tp")),
        P(("exp", "tp"), "seq"),
        P(("seq", "exp"), "tp"),
    )
    out_specs = (
        P(("seq", "exp"), "tp"),
        P("seq", ("exp", "tp")),
        P("seq", ("exp", "tp")),
        P(("exp", "tp"), "seq"),
    )
    return jax.shard_map(body, mesh=mesh, in_specs=in_specs, out_specs=out_specs, check_vma=False)
```

```python
import jax
import jax.numpy as jnp
from jax import lax
from jax.experimental import pallas as pl
from jax.experimental.pallas import tpu as pltpu
from jax.sharding import PartitionSpec as P

MESH = pl.DeviceIdType.MESH
F32 = jnp.float32
BF16 = jnp.bfloat16
Z_ORDER = (0, 1, 7, 2, 6, 3, 5, 4)
Z_POS = {z: i for i, z in enumerate(Z_ORDER)}
N_RECV = 280
N_SEND = 40


WAVES = ((0, 160), (320, 96))
Z_FIRST = 640


def row_at(pos, other=0):
    return other * 160 + pos * 32 if pos < 5 else 320 + other * 96 + (pos - 5) * 32


def row_of(z, other=0):
    return row_at(Z_POS[z % 8], other)


def sigmoid(a):
    return 1.0 / (1.0 + jnp.exp(-a))


class Agenda:
    def __init__(self):
        self.steps = []

    def at(self, time, step):
        self.steps.append((time, len(self.steps), step))

    def run(self):
        for _, _, step in sorted(self.steps, key=lambda s: (s[0], s[1])):
            step()


def kernel(
    tokens, ids, weights, egate, eup, edown, sgate, sup, sdown, ograd,
    t_hbm, gg_hbm, gu_hbm, gd_hbm,
    tok, act, dout, wt, wed, wgu, wd, hid, coef, part, sibp, rsb, gu, hg, gt, grad, ring, t_out, gg_out, gu_out, gd_out, ids_v, weights_v,
    send_sems, recv_sems, local_sems,
):
    yo = lax.axis_index("seq")
    eo = lax.axis_index("exp")
    xo = lax.axis_index("tp")
    zo = eo // 2
    co = lax.rem(eo, 2)

    def z_dev(d):
        return (yo, lax.rem(zo + d + 8, 8) * 2 + co, xo)

    def x_dev(d):
        return (yo, eo, lax.rem(xo + d + 4, 4))

    def y_dev(d):
        return (lax.rem(yo + d + 8, 8), eo, xo)

    sib = (yo, zo * 2 + (1 - co), xo)
    agenda = Agenda()
    drains = []
    counts = {"send": 0, "recv": 0, "local": 0}

    def new_send():
        counts["send"] += 1
        assert counts["send"] <= N_SEND
        return send_sems.at[counts["send"] - 1]

    def new_recv():
        counts["recv"] += 1
        assert counts["recv"] <= N_RECV
        return recv_sems.at[counts["recv"] - 1]

    def send(src, dst, s_sem, r_sem, device):
        pltpu.make_async_remote_copy(
            src_ref=src, dst_ref=dst, send_sem=s_sem, recv_sem=r_sem,
            device_id=device, device_id_type=MESH,
        ).start()

    def wait_recv(ref, r_sem):
        pltpu.make_async_remote_copy(
            src_ref=ref, dst_ref=ref, send_sem=send_sems.at[0], recv_sem=r_sem,
            device_id=sib, device_id_type=MESH,
        ).wait_recv()

    def drain(ref, s_sem):
        def step():
            pltpu.make_async_remote_copy(
                src_ref=ref, dst_ref=ref, send_sem=s_sem, recv_sem=recv_sems.at[0],
                device_id=sib, device_id_type=MESH,
            ).wait_send()

        drains.append(step)

    barrier = pltpu.get_barrier_semaphore()
    peers = [z_dev(d) for d in range(1, 8)] + [x_dev(d) for d in range(1, 4)] + [y_dev(1), y_dev(-1), sib]
    for device in peers:
        pl.semaphore_signal(barrier, inc=1, device_id=device, device_id_type=MESH)

    local = []

    def load(src, dst):
        copy = pltpu.make_async_copy(src, dst, local_sems.at[len(local)])
        copy.start()
        local.append(copy)
        return copy

    blocks = [
        load(tokens, tok.at[0, pl.ds(0, 32)]),
        load(sgate, wgu.at[pl.ds(pl.multiple_of(yo * 512, 512), 512), pl.ds(0, 128)]),
        load(sup, wgu.at[pl.ds(pl.multiple_of(yo * 512, 512), 512), pl.ds(128, 128)]),
        load(sdown, wd.at[yo]),
        load(ograd, dout.at[0, pl.ds(0, 32)]),
    ]
    routes = [load(ids, ids_v), load(weights, weights_v)]
    stores = []

    def store(i, src, dst):
        copy = pltpu.make_async_copy(src, dst, local_sems.at[10 + i])
        copy.start()
        stores.append(copy)

    later = [
        load(egate.at[0], wt.at[:, pl.ds(0, 128)]),
        load(eup.at[0], wt.at[:, pl.ds(128, 128)]),
        load(edown.at[0], wed),
    ]

    pl.semaphore_wait(barrier, len(peers))
    blocks[0].wait()

    def gather(buf, t0, times=None):
        s_z0, s_x0, s_f0, s_b0 = new_send(), [new_send() for _ in range(2)], new_send(), new_send()
        s_x2, s_x1, s_z1, s_b1 = new_send(), new_send(), new_send(), new_send()
        pieces = ((0, 1), (1, 2), (3, 2), (5, 2), (7, 1))
        r_z0 = {(d, k): new_recv() for d in "RL" for k in range(1, 5)}
        r_x0 = {(rel, k): new_recv() for rel in (1, 3) for k in range(5)}
        r_f0 = {(rel, k): new_recv() for rel in (1, 3) for k in range(4)}
        r_x2 = new_recv()
        r_x1 = {rel: new_recv() for rel in (1, 2, 3)}
        r_z1 = {(d, k, c): new_recv() for d in "RL" for k in range(1, 5) for c in range(4)}
        r_b0, r_b1 = [new_recv() for _ in range(2)], [new_recv() for _ in range(2)]
        cols0, cols1 = pl.ds(0, Z_FIRST), pl.ds(Z_FIRST, 1024 - Z_FIRST)
        part_cols = {"R": pl.ds(0, 384), "L": pl.ds(384, Z_FIRST - 384)}

        def came(d, k):
            return (8 - k) % 8 if d == "R" else k % 8

        def z0_ref(z, d, k):
            return buf.at[0, pl.ds(row_of(z), 32), part_cols[d] if k == 4 else cols0]

        def z0_send(d, k, reach):
            device = z_dev(reach if d == "R" else -reach)
            send(z0_ref(came(d, k - reach), d, k), z0_ref(came(d, k), d, k), s_z0, r_z0[d, k], device)

        def piece_ref(rel, k, cols=cols0, other=0):
            pos, n = pieces[k]
            return buf.at[rel, pl.ds(row_at(pos, other), 32 * n), cols]

        def x0_piece(k):
            for i, d in enumerate((1, -1)):
                send(piece_ref(0, k), piece_ref((-d) % 4, k), s_x0[i], r_x0[(-d) % 4, k], x_dev(d))
            if k == 4:
                send(piece_ref(0, k), piece_ref(2, k), s_x2, r_x2, x_dev(2))

        def z1_ref(z, c):
            return buf.at[c, pl.ds(row_of(z), 32), cols1]

        def z1_send(d, k, c, reach=1):
            device = z_dev(reach if d == "R" else -reach)
            send(z1_ref(came(d, k - reach), c), z1_ref(came(d, k), c), s_z1, r_z1[d, k, c], device)

        def b0_send(rel, k):
            send(piece_ref(rel, k), piece_ref(rel, k, other=1), s_b0, r_b0[0 if k < 3 else 1], sib)

        def b1_send(z):
            send(
                buf.at[:, pl.ds(row_of(z), 32), cols1],
                buf.at[:, pl.ds(row_of(z, 1), 32), cols1],
                s_b1, r_b1[0 if Z_POS[z] < 5 else 1], sib,
            )

        plan = {("begin",): 0.0, ("x1",): 2.95, ("ready", 0): 12.24, ("ready", 1): 16.6}
        for k, (here, start, there, beyond) in enumerate(
            ((0, 0.01, 3.3, 11.6), (2.9, 2.91, 6.5, 11.6), (4.2, 4.21, 8.35, 12.0), (8.4, 8.41, 11.4, 15.3), (9.45, 9.46, 12.15, 15.35))
        ):
            plan["x0", k], plan["x0_done", k], plan["f0_done", k] = start, there, beyond
            if k:
                plan["z0", k] = here
                for c, when in ((0, 0.2 if k < 2 else 0.65), (1, 2.5), (3, 3.0), (2, 3.5)):
                    plan["z1", k, c] = 2.9 * k + when
        plan.update(times or {})

        def at(name, step):
            agenda.at(t0 + plan[name], step)

        def begin():
            for d in (1, -1, 2):
                send(z1_ref(0, 0), z1_ref(0, (-d) % 4), s_x1, r_x1[(-d) % 4], x_dev(d))
            for d in "RL":
                z0_send(d, 1, 1)
                z0_send(d, 2, 2)
            for d in "RL":
                z1_send(d, 1, 0)

        at(("begin",), begin)

        def z0_hop(k):
            for d in "RL":
                wait_recv(z0_ref(came(d, k), d, k), r_z0[d, k])
                if k == 2:
                    z0_send(d, 3, 1)
                    z0_send(d, 4, 2)

        def x0_start(k):
            x0_piece(k)
            b0_send(0, k)

        for k in range(1, 5):
            at(("z0", k), lambda k=k: z0_hop(k))
        for k in range(5):
            at(("x0", k), lambda k=k: x0_start(k))

        def x0_done(rel, k):
            wait_recv(piece_ref(rel, k), r_x0[rel, k])
            if k < 4:
                d, way = (1, "R") if rel == 3 else (-1, "L")
                send(
                    piece_ref(rel, k, part_cols[way]), piece_ref(2, k, part_cols[way]),
                    s_f0, r_f0[rel, k], x_dev(d),
                )
            b0_send(rel, k)

        def f0_done(k):
            if k == 4:
                wait_recv(piece_ref(2, k), r_x2)
            else:
                for rel, way in ((3, "R"), (1, "L")):
                    wait_recv(piece_ref(2, k, part_cols[way]), r_f0[rel, k])
            b0_send(2, k)

        for k in range(5):
            for rel in (1, 3):
                at(("x0_done", k), lambda rel=rel, k=k: x0_done(rel, k))
            at(("f0_done", k), lambda k=k: f0_done(k))

        def x1_done(rel):
            wait_recv(z1_ref(0, rel), r_x1[rel])
            for d in "RL":
                z1_send(d, 1, rel)
            if rel == 2:
                b1_send(0)

        for rel in (1, 3, 2):
            at(("x1",), lambda rel=rel: x1_done(rel))

        def z1_hop(k, c):
            for d in "RL":
                if k == 4 and (d == "R") != (c in (0, 1)):
                    continue
                z = came(d, k)
                wait_recv(z1_ref(z, c), r_z1[d, k, c])
                if k < 3:
                    z1_send(d, k + 1, c)
                if k == (2 if times is None else 3) and (d == "R") == (c in (0, 1)):
                    z1_send(d, 4, c, 4 - k)
                if c == 2:
                    b1_send(z)

        for k in range(1, 5):
            for c in (0, 1, 3, 2):
                at(("z1", k, c), lambda k=k, c=c: z1_hop(k, c))

        def finish(wave):
            first, n = WAVES[wave]
            rows = pl.ds(first + n, n)
            wait_recv(buf.at[:, rows, cols0], r_b0[wave])
            wait_recv(buf.at[:, rows, cols1], r_b1[wave])

        for wave in range(2):
            at(("ready", wave), lambda wave=wave: finish(wave))
        drain(buf.at[0, pl.ds(0, 224), cols0], s_z0)
        for sem in s_x0:
            drain(buf.at[0, pl.ds(0, 256), cols0], sem)
        drain(buf.at[0, pl.ds(0, 224), cols0], s_f0)
        drain(buf.at[0, pl.ds(0, 32), cols0], s_x2)
        drain(buf.at[:, pl.ds(0, 256), cols0], s_b0)
        drain(buf.at[pl.ds(1, 3), pl.ds(0, 32), cols1], s_x1)
        drain(buf.at[:, pl.ds(0, 224), cols1], s_z1)
        drain(buf.at[:, pl.ds(0, 256), cols1], s_b1)
        return [t0 + plan["ready", 0], t0 + plan["ready", 1]]

    s_yw = [new_send() for _ in range(3)]
    r_yw = {(d, k, a): new_recv() for d in "RL" for k in range(1, 5) for a in range(3)}

    def yw_ref(a, origin, d, k):
        if a < 2:
            start, n = origin * 512, 512
            if k == 4:
                start, n = start + (0 if d == "R" else 256), 256
            return wgu.at[pl.ds(pl.multiple_of(start, 256), n), pl.ds(a * 128, 128)]
        if k == 4:
            return wd.at[origin, pl.ds(0 if d == "R" else 64, 64)]
        return wd.at[origin]

    def yw_origin(d, k):
        return lax.rem(yo + (8 - k if d == "R" else k), 8)

    def yw_send(d, k, a):
        ref = yw_ref(a, yw_origin(d, k - 1), d, k)
        send(ref, ref, s_yw[a], r_yw[d, k, a], y_dev(1 if d == "R" else -1))

    def yw_start():
        for copy in blocks[1:]:
            copy.wait()
        for a in range(3):
            for d in "RL":
                yw_send(d, 1, a)

    def yw_hop(k, a):
        for d in "RL":
            wait_recv(yw_ref(a, yw_origin(d, k), d, k), r_yw[d, k, a])
            if k < 4:
                yw_send(d, k + 1, a)

    agenda.at(0.01, yw_start)
    yw_times = ((5.6, 6.1, 8.6), (11.4, 12.35, 13.46), (16.62, 20.35, 23.11), (25.46, 26.05, 26.65))
    for k in range(1, 5):
        for a in range(3):
            agenda.at(yw_times[k - 1][a], lambda k=k, a=a: yw_hop(k, a))
    drain(wgu.at[pl.ds(0, 3584), pl.ds(0, 128)], s_yw[0])
    drain(wgu.at[pl.ds(0, 3584), pl.ds(128, 128)], s_yw[1])
    drain(wd.at[pl.ds(0, 7)], s_yw[2])

    s_co, s_cb = new_send(), new_send()
    r_co = {z: new_recv() for z in range(1, 8)}
    r_cb = new_recv()

    def coef_start():
        for copy in routes:
            copy.wait()
        lane = lax.broadcasted_iota(jnp.int32, (16, 128), 1)
        lane_e = lax.rem(lane, 16)
        lane_half = lax.rem(lane // 16, 2)
        blank = jnp.zeros((8, 96), jnp.int32)
        names = jnp.concatenate([ids_v[...], blank], axis=1).T
        shares = jnp.concatenate([weights_v[...], blank.astype(F32)], axis=1).T
        halves = []
        for half in range(2):
            total = jnp.zeros((16, 128), F32)
            for k in range(8):
                name = names[half * 16 : half * 16 + 16, k : k + 1]
                weight = shares[half * 16 : half * 16 + 16, k : k + 1]
                total = total + jnp.where(lane_e == name, weight, 0.0)
            halves.append(total)
        value = jnp.where(lane_half == 0, halves[0], halves[1])
        high = value.astype(BF16).astype(F32)
        value = jnp.where(lane < 32, high, jnp.where(lane < 64, value - high, 0.0))
        coef[0, 0] = value.astype(BF16)
        for z in range(1, 8):
            send(coef.at[0, 0], coef.at[0, Z_POS[8 - z]], s_co, r_co[8 - z], z_dev(z))

    def coef_mirror():
        for z in range(1, 8):
            wait_recv(coef.at[0, Z_POS[z]], r_co[z])
        send(coef.at[0], coef.at[1], s_cb, r_cb, sib)

    agenda.at(4.0, coef_start)
    agenda.at(16.0, coef_mirror)
    drain(coef.at[0, pl.ds(0, 7)], s_co)
    drain(coef.at[0], s_cb)

    t_tok = gather(tok, 0.0)
    late = {("begin",): 12.22, ("x1",): 16.55, ("ready", 0): 35.2, ("ready", 1): 35.21}
    for k, (when, start, there, beyond) in enumerate(
        ((0, 16.69, 23.12, 35.13), (16.56, 20.3, 25.45, 35.13), (16.68, 22.96, 26.6, 35.13), (25.41, 25.42, 26.7, 35.13), (25.41, 25.43, 26.8, 35.13))
    ):
        late["x0", k], late["x0_done", k], late["f0_done", k] = start, there, beyond
        if k:
            late["z0", k] = when
            for c in range(4):
                late["z1", k, c] = (20.5, 23.1, 26.5, 35.12)[k - 1]
    gather(dout, 0.0, late)

    def weight_wait():
        for copy in later:
            copy.wait()

    agenda.at(t_tok[0] + 0.01, weight_wait)
    s_hid = [new_send() for _ in range(2)]
    r_hid = {(d, w, other): new_recv() for d in (1, 2, 3) for w in range(2) for other in range(2)}

    def hid_cols(d):
        return pl.ds(pl.multiple_of(lax.rem(xo + d, 4) * 128, 128), 128)

    def project(buf, w, rows, out):
        out[rows, :] = jnp.dot(
            buf[0, rows, :],
            w[pl.ds(pl.multiple_of(xo * 1024, 1024), 1024), :],
            preferred_element_type=F32,
        )

        @pl.loop(1, 4)
        def _(rel):
            chunk = lax.rem(xo + rel, 4)
            out[rows, :] += jnp.dot(
                buf[rel, rows, :],
                w[pl.ds(pl.multiple_of(chunk * 1024, 1024), 1024), :],
                preferred_element_type=F32,
            )

    def wave_rows(wave):
        first, n = WAVES[wave]
        return pl.ds(first, 2 * n)

    def teacher_hidden(wave):
        rows = wave_rows(wave)
        project(tok, wt, rows, gu)
        gate = gu[rows, 0:128]
        up = gu[rows, 128:256]
        hid[rows, hid_cols(0)] = (gate * sigmoid(gate) * up).astype(BF16)
        first, n = WAVES[wave]
        for other in (1, 0):
            ref = hid.at[pl.ds(first + other * n, n), hid_cols(0)]
            for d in (1, 3, 2):
                send(ref, ref, s_hid[wave], r_hid[4 - d, wave, other], x_dev(d))

    for wave in range(2):
        agenda.at(t_tok[wave] + 0.02, lambda wave=wave: teacher_hidden(wave))
        drain(hid.at[wave_rows(wave), pl.ds(0, 384)], s_hid[wave])

    s_sp = [new_send() for _ in range(2)]
    r_sp = [new_recv() for _ in range(2)]
    s_rs = new_send()
    r_rs = {z: new_recv() for z in (1, 7)}
    r_rs.update({(z, turn): new_recv() for z in (2, 3, 5, 6) for turn in range(2)})
    r_rs4 = [new_recv() for _ in range(2)]

    def coef_column(other, wave):
        start, n = ((0, 5), (5, 3))[wave]
        lanes = lax.broadcasted_iota(jnp.int32, (n, 16, 128), 2)
        rows = coef[other, start : start + n].astype(F32)
        cols = []
        for half in range(2):
            wanted = (lanes == half * 16 + eo) | (lanes == 32 + half * 16 + eo)
            cols.append(jnp.sum(jnp.where(wanted, rows, 0.0), axis=2, keepdims=True))
        return jnp.concatenate(cols, axis=1).reshape(n * 32, 1)

    def hid_wait(wave):
        if wave == 0:
            wait_recv(coef.at[1], r_cb)

    def teacher_down(wave, other):
        first, n = WAVES[wave]
        rows = pl.ds(first + other * n, n)
        own = pl.ds(first, n)
        scale = coef_column(other, wave)
        for d in (1, 3, 2):
            wait_recv(hid.at[rows, hid_cols(d)], r_hid[d, wave, other])
        if other == 0:
            wait_recv(sibp.at[own], r_sp[wave])
        for q in range(2):
            cols = slice(q * 512, q * 512 + 512)
            res = jnp.dot(hid[rows, :], wed[:, cols], preferred_element_type=F32) * scale
            if other == 0:
                res = res + sibp[own, cols].astype(F32)
            part[rows, cols] = res.astype(BF16)
        if other == 1:
            send(part.at[rows], sibp.at[own], s_sp[wave], r_sp[wave], sib)
        else:
            if wave == 0:
                for z in (1, 7):
                    send(part.at[pl.ds(row_of(z), 32)], rsb.at[8 - z], s_rs, r_rs[8 - z], z_dev(z))
            else:
                for turn in range(2):
                    for z, step, i in ((3, 1, 0), (5, -1, 1)):
                        half = pl.ds(512 * (i ^ 1 ^ turn), 512)
                        send(
                            part.at[pl.ds(row_of(z), 32), half], rsb.at[8 - z, :, half],
                            s_rs, r_rs[8 - z, turn], z_dev(step),
                        )
                        if turn == 0:
                            half = pl.ds(512 * i, 512)
                            send(
                                part.at[pl.ds(row_of(4), 32), half], rsb.at[4, :, half],
                                s_rs, r_rs4[i], z_dev(2 * step),
                            )

    t_down = [20.2, 22.9]
    for wave in range(2):
        agenda.at(t_down[wave], lambda wave=wave: hid_wait(wave))
        for other in (1, 0):
            agenda.at(
                t_down[wave] + (0.1, 2.1)[1 - other],
                lambda wave=wave, other=other: teacher_down(wave, other),
            )
        first, n = WAVES[wave]
        drain(part.at[pl.ds(first + n, n)], s_sp[wave])
    drain(part.at[pl.ds(0, 224)], s_rs)

    def teacher_relay(turn):
        for i, (z, far) in enumerate(((2, 5), (6, 3))):
            start = 512 * (i ^ 1 ^ turn)
            half = pl.ds(start, 512)
            rows = pl.ds(row_of(z), 32)
            wait_recv(rsb.at[far, :, half], r_rs[far, turn])
            total = part[rows, half].astype(F32) + rsb[far, :, half].astype(F32)
            if turn == 1:
                wait_recv(rsb.at[4, :, half], r_rs4[i])
                total = total + rsb[4, :, half].astype(F32)
            part[rows, half] = total.astype(BF16)
            send(part.at[rows, half], rsb.at[8 - z, :, half], s_rs, r_rs[8 - z, turn], z_dev(z))

    for turn in range(2):
        agenda.at(26.0 + 0.1 * turn, lambda turn=turn: teacher_relay(turn))

    def teacher_sum():
        total = part[0:32, :].astype(F32)
        for z in (1, 7, 2, 6):
            if z in (1, 7):
                wait_recv(rsb.at[z], r_rs[z])
            else:
                for turn in range(2):
                    half = pl.ds(512 * ((0 if z == 6 else 1) ^ 1 ^ turn), 512)
                    wait_recv(rsb.at[z, :, half], r_rs[z, turn])
            total = total + rsb[z].astype(F32)
        row = total.astype(BF16)
        t_out[...] = row
        store(0, t_out, t_hbm)
        act[0, 0:32, :] = row

    t_sum = 35.0
    agenda.at(t_sum, teacher_sum)

    def student_back(rel):
        chunk = lax.rem(xo + rel, 4)
        total = jnp.zeros((512, 128), F32) if rel == 0 else hg[...]
        for j in range(2):
            total = total + lax.dot_general(
                dout[rel, :, j * 512 : j * 512 + 512],
                wd[chunk * 2 + j],
                (((1,), (1,)), ((), ())),
                preferred_element_type=F32,
            )
        hg[...] = total

    t_act = gather(act, t_sum + 0.1)
    for rel, when in enumerate((0.2, 0.2, 6.55, 6.55)):
        agenda.at(t_sum + 0.1 + when, lambda rel=rel: student_back(rel))

    def student_rows(wave):
        first, n = WAVES[wave]
        rows = pl.ds(first, 2 * n)
        project(act, wgu, rows, gu)
        gate = gu[rows, 0:128]
        up = gu[rows, 128:256]
        back = hg[rows, :]
        sig = sigmoid(gate)
        silu = gate * sig
        terms = (back * up * (sig * (1.0 + gate * (1.0 - sig))), back * silu, silu * up)
        for i, term in enumerate(terms):
            gt[i * 128 : i * 128 + 128, rows] = term.T.astype(BF16)

    for wave in range(2):
        agenda.at(t_act[wave] + 0.1, lambda wave=wave: student_rows(wave))

    s_yg = [new_send() for _ in range(3)]
    r_yg = {(d, k, a): new_recv() for d in "RL" for k in range(4) for a in range(3)}

    def term(k, a):
        owner = lax.rem(yo + k, 8)
        rel = lax.rem(owner // 2 - xo + 4, 4)
        cols = pl.ds(pl.multiple_of(lax.rem(owner, 2) * 512, 512), 512)
        if a == 0:
            grad[k, 0:256, :] = jnp.dot(
                gt[0:256, :], act[rel, :, cols], preferred_element_type=F32
            ).astype(BF16)
        else:
            grad[k, 256:384, :] = jnp.dot(
                gt[256:384, :], dout[rel, :, cols], preferred_element_type=F32
            ).astype(BF16)

    def yg_ref(d, k, a):
        if k == 0:
            return ring.at[0 if d == "R" else 1, 0, a, pl.ds(0 if d == "R" else 64, 64)]
        return ring.at[0 if d == "R" else 1, k, a]

    def yg_send(d, k, a):
        if k == 0:
            src = grad.at[4, pl.ds(a * 128 + (0 if d == "R" else 64), 64)]
        else:
            src = grad.at[4 - k if d == "R" else 4 + k, pl.ds(a * 128, 128)]
        send(src, yg_ref(d, k, a), s_yg[a], r_yg[d, k, a], y_dev(1 if d == "R" else -1))

    t_g = t_act[1] + 1.0

    def first_terms():
        term(4, 0)
        for a in range(2):
            for d in "RL":
                yg_send(d, 0, a)
        term(4, 1)
        for d in "RL":
            yg_send(d, 0, 2)
        for k in (3, 5):
            for a in range(2):
                term(k, a)

    agenda.at(t_g, first_terms)
    for i, k in enumerate((2, 6, 1, 7, 0)):
        for a in range(2):
            agenda.at(t_g + 8.0 + 3.2 * i + 1.5 * a, lambda k=k, a=a: term(k, a))

    def yg_hop(k, a):
        for d in "RL":
            wait_recv(yg_ref(d, k - 1, a), r_yg[d, k - 1, a])
            way = 0 if d == "R" else 1
            mine = 4 - k if d == "R" else 4 + k
            lo, n = a * 128, 128
            off = 0
            if k == 1:
                off, n = (0, 64) if d == "R" else (64, 64)
            grad[mine, lo + off : lo + off + n, :] = (
                grad[mine, lo + off : lo + off + n, :].astype(F32)
                + ring[way, k - 1, a, off : off + n, :].astype(F32)
            ).astype(BF16)
            yg_send(d, k, a)

    for k in range(1, 4):
        for a in range(3):
            agenda.at(t_g + 3.0 + 8.9 * (k - 1) + 2.95 * a, lambda k=k, a=a: yg_hop(k, a))

    def yg_last(a):
        for d in "RL":
            wait_recv(yg_ref(d, 3, a), r_yg[d, 3, a])
        total = (
            grad[0, a * 128 : a * 128 + 128, :].astype(F32)
            + ring[0, 3, a].astype(F32)
            + ring[1, 3, a].astype(F32)
        )
        if a == 0:
            gg_out[...] = total.T
            store(1, gg_out, gg_hbm)
        elif a == 1:
            gu_out[...] = total.T
            store(2, gu_out, gu_hbm)
        else:
            gd_out[...] = total
            store(3, gd_out, gd_hbm)

    for a in range(3):
        agenda.at(t_g + 3.0 + 8.9 * 3 + 2.95 * a, lambda a=a: yg_last(a))
        drain(grad.at[pl.ds(1, 7), pl.ds(a * 128, 128)], s_yg[a])

    agenda.run()
    for step in drains:
        step()
    for copy in stores:
        copy.wait()


def hand_over(*refs):
    ins, outs, held, sems = refs[:4], refs[4:8], refs[8:12], refs[12]
    loads = [pltpu.make_async_copy(ins[i], held[i], sems.at[i]) for i in range(4)]
    writes = [pltpu.make_async_copy(held[i], outs[i], sems.at[4 + i]) for i in range(4)]
    for load in loads:
        load.start()
    for load, write in zip(loads, writes):
        load.wait()
        write.start()
    for write in writes:
        write.wait()


def body(*args):
    any_spec = pl.BlockSpec(memory_space=pl.ANY)
    scratch = [
        pltpu.VMEM((4, 512, 1024), BF16),
        pltpu.VMEM((4, 512, 1024), BF16),
        pltpu.VMEM((4, 512, 1024), BF16),
        pltpu.VMEM((4096, 256), BF16),
        pltpu.VMEM((512, 1024), BF16),
        pltpu.VMEM((4096, 256), BF16),
        pltpu.VMEM((8, 128, 512), BF16),
        pltpu.VMEM((512, 512), BF16),
        pltpu.VMEM((2, 8, 16, 128), BF16),
        pltpu.VMEM((512, 1024), BF16),
        pltpu.VMEM((512, 1024), BF16),
        pltpu.VMEM((8, 32, 1024), BF16),
        pltpu.VMEM((512, 256), F32),
        pltpu.VMEM((512, 128), F32),
        pltpu.VMEM((384, 512), BF16),
        pltpu.VMEM((8, 384, 512), BF16),
        pltpu.VMEM((2, 4, 3, 128, 512), BF16),
        pltpu.VMEM((32, 1024), BF16),
        pltpu.VMEM((512, 128), F32),
        pltpu.VMEM((512, 128), F32),
        pltpu.VMEM((128, 512), F32),
        pltpu.VMEM((8, 32), jnp.int32),
        pltpu.VMEM((8, 32), F32),
        pltpu.SemaphoreType.DMA((N_SEND,)),
        pltpu.SemaphoreType.DMA((N_RECV,)),
        pltpu.SemaphoreType.DMA((14,)),
    ]
    shapes = (
        jax.ShapeDtypeStruct((32, 1024), BF16),
        jax.ShapeDtypeStruct((512, 128), F32),
        jax.ShapeDtypeStruct((512, 128), F32),
        jax.ShapeDtypeStruct((128, 512), F32),
    )
    results = pl.pallas_call(
        kernel,
        out_shape=shapes,
        in_specs=[any_spec] * 10,
        out_specs=(any_spec,) * 4,
        scratch_shapes=scratch,
        compiler_params=pltpu.CompilerParams(
            collective_id=1, has_side_effects=True, vmem_limit_bytes=62 * 1024 * 1024
        ),
        cost_estimate=pl.CostEstimate(flops=5_000_000_000, bytes_accessed=12_000_000, transcendentals=400_000),
        name="distill_window",
    )(args[0], args[1].T, args[2].T, *args[3:])
    return pl.pallas_call(
        hand_over,
        out_shape=shapes,
        in_specs=[any_spec] * 4,
        out_specs=(any_spec,) * 4,
        scratch_shapes=[pltpu.VMEM(shape.shape, shape.dtype) for shape in shapes] + [pltpu.SemaphoreType.DMA((8,))],
        compiler_params=pltpu.CompilerParams(vmem_limit_bytes=62 * 1024 * 1024),
        cost_estimate=pl.CostEstimate(flops=0, bytes_accessed=1_700_000, transcendentals=0),
        name="hand_over",
    )(*results)


def solution(mesh):
    in_specs = (
        P(("seq", "exp"), "tp"),
        P(("seq", "exp"), None),
        P(("seq", "exp"), None),
        P("exp", None, "tp"),
        P("exp", None, "tp"),
        P("exp", None, "tp"),
        P("seq", ("exp", "tp")),
        P("seq", ("exp", "tp")),
        P(("exp", "tp"), "seq"),
        P(("seq", "exp"), "tp"),
    )
    out_specs = (
        P(("seq", "exp"), "tp"),
        P("seq", ("exp", "tp")),
        P("seq", ("exp", "tp")),
        P(("exp", "tp"), "seq"),
    )
    return jax.shard_map(body, mesh=mesh, in_specs=in_specs, out_specs=out_specs, check_vma=False)
```
